32 devices in a mesh: dp: 8 (over z, y), mp: 4 (over x, core).
Axes of the slice: x: 2, y: 2, z: 4, core: 2. Of those that a mesh axis runs over, the one named last changes fastest.
Arguments:
- hidden_states: bfloat16 [4096, 3584], P('dp'), may hold values from -6 to 6
- token_ids: int32 [256, 16], P('dp'), may hold values from 0 to 152063, as said below
- norm_gain: float32 [3584], replicated, may hold values from 0.5 to 1.5
- q_weight: bfloat16 [3584, 3584], P('dp', 'mp'), may hold values from -0.09375 to 0.09375
- key_matrix: bfloat16 [3584, 512], P('dp', 'mp'), may hold values from -0.09375 to 0.09375
- value_matrix: bfloat16 [3584, 512], P('dp', 'mp'), may hold values from -0.09375 to 0.09375
- out_weight: bfloat16 [3584, 3584], P('dp', 'mp'), may hold values from -0.09375 to 0.09375
- label_table: bfloat16 [8192, 3584], P(('dp', 'mp')), may hold values from -6 to 6
- refresh_rows: int32 [256], P(('dp', 'mp')), may hold values from 0 to 255, as said below
- label_counts: int32 [8192], P(('dp', 'mp')), may hold values from 1 to 8191
- queries: bfloat16 [128, 3584], replicated, may hold values from -6 to 6
- positives: int32 [128, 8], replicated, may hold values from 0 to 8191
Outputs:
- label_grad: float32 [8192, 3584], P(('dp', 'mp'))
- query_grad: float32 [128, 3584], replicated
- loss: float32 [], replicated
The draws below stay inside these ranges and needn't reach their ends.
Inputs may be any that keep to these rules, and one draw needn't show every extreme that they name: `token_ids`: in every text the first id is not 0, and after an id 0 all later ids of that text are 0. `refresh_rows`: the 8 entries of each aligned block of 8 entries are distinct.
All inputs are finite; a program needn't handle non-finite values.
Results may differ from the reference program's by a relative error of at most 0.003.
Values may be sent and summed in bfloat16 or wider, within the bound.
A program may use at most 128 MiB of HBM per device.

```python
import math
import jax
import jax.numpy as jnp
from jax import lax

MODEL_WIDTH = 3584
HQ = 28
KEY_VALUE_HEADS = 4
HEAD_WIDTH = 128
VOCAB = 152064
TXT = 16
POS = 8
LAB_GRP = 32
LAB_OWN = 256
BATCH = 128
TEXTS = 256
TOKENS = 4096
REF = 8
LABELS = 8192
N_DP = 8


def draw_token_ids(key, part):
    first_key, second_key = jax.random.split(key)
    lengths = jax.random.randint(first_key, (TEXTS, 1), 1, TXT + 1)
    values = jax.random.randint(second_key, (TEXTS, TXT), 1, VOCAB)
    places = jnp.arange(TXT, dtype=jnp.int32)[None, :]
    return jnp.where(places < lengths, values, 0).astype(jnp.int32)


def draw_refresh_rows(key, part):
    blocks = TEXTS // REF
    keys = jax.random.split(key, blocks)
    selected_rows = jax.vmap(lambda block_key: jax.random.permutation(block_key, LAB_OWN)[:REF])(keys)
    return selected_rows.reshape(-1).astype(jnp.int32)


def draw_label_counts(key, part):
    first_key, second_key = jax.random.split(key)
    places = jnp.arange(LABELS, dtype=jnp.int32)
    ceiling = 2 + 12 * places // LABELS
    exponent = jax.random.randint(first_key, (LABELS,), 0, 1 << 20) % ceiling
    power = jnp.left_shift(jnp.ones((LABELS,), jnp.int32), exponent)
    extra = jax.random.randint(second_key, (LABELS,), 0, 1 << 20) % power
    counts = power + extra
    counts = jnp.where(places == 0, 1, counts)
    counts = jnp.where(places == LABELS - 1, 8191, counts)
    return counts.astype(jnp.int32)


def with_ends(array, rng, low, top_value):
    dims = array.shape
    index_at = [jax.random.randint(jax.random.fold_in(rng, axis), (), 0, dims[axis]) for axis in range(len(dims))]
    array = array.at[tuple(index_at)].set(low)
    longest = dims.index(max(dims))
    index_at[longest] = (index_at[longest] + 1) % dims[longest]
    return array.at[tuple(index_at)].set(top_value)


def levels(key, extent, pieces, low, largest):
    level, own = 1.0, jax.random.fold_in(key, 6)
    for position, parts in pieces:
        steps = jnp.exp(jax.random.uniform(jax.random.fold_in(own, position), (parts,), jnp.float32, low / len(pieces), largest / len(pieces)))
        level = level * jnp.repeat(steps, extent[position] // parts).reshape([-1 if axis == position else 1 for axis in range(len(extent))])
    return level


def scatter_about(stream_key, dims, deviation, limit, cuts=(), held_as=jnp.bfloat16):
    result = jax.random.normal(stream_key, dims, jnp.float32) * deviation
    if len(cuts) > 0:
        result = levels(stream_key, dims, cuts, -0.22, 0.18) * result
    return jnp.clip(result, min=-limit, max=limit).astype(held_as)


def setup_inputs(seed: int = 0) -> dict:
    arg_keys = jax.random.split(jax.random.key(seed), 13)
    hidden_states = scatter_about(arg_keys[0], (TOKENS, MODEL_WIDTH), 1.0, 6.0, ((0, 8),))
    token_ids = draw_token_ids(jax.random.fold_in(arg_keys[12], 71), 0)
    norm_gain = jnp.clip(1.0 + 0.1 * jax.random.normal(arg_keys[2], (MODEL_WIDTH,), jnp.float32), 0.5, 1.5)
    q_weight = scatter_about(arg_keys[3], (MODEL_WIDTH, HQ * HEAD_WIDTH), MODEL_WIDTH ** -0.5, 0.09375, ((0, 8), (1, 4)))
    key_matrix = scatter_about(arg_keys[4], (MODEL_WIDTH, KEY_VALUE_HEADS * HEAD_WIDTH), MODEL_WIDTH ** -0.5, 0.09375, ((0, 8), (1, 4)))
    value_matrix = scatter_about(arg_keys[5], (MODEL_WIDTH, KEY_VALUE_HEADS * HEAD_WIDTH), MODEL_WIDTH ** -0.5, 0.09375, ((0, 8), (1, 4)))
    out_weight = scatter_about(arg_keys[6], (MODEL_WIDTH, HQ * HEAD_WIDTH), (HQ * HEAD_WIDTH) ** -0.5, 0.09375, ((0, 8), (1, 4)))
    label_table = scatter_about(arg_keys[7], (LABELS, MODEL_WIDTH), 1.0, 6.0, ((0, 32),))
    refresh_rows = draw_refresh_rows(jax.random.fold_in(arg_keys[12], 71), 0)
    label_counts = draw_label_counts(jax.random.fold_in(arg_keys[12], 71), 0)
    queries = scatter_about(arg_keys[10], (BATCH, MODEL_WIDTH), 1.0, 6.0)
    positives = with_ends(jax.random.randint(arg_keys[11], (BATCH, POS), 0, LABELS), jax.random.fold_in(arg_keys[11], 1), 0, LABELS - 1).astype(jnp.int32)
    return dict(hidden_states=hidden_states, token_ids=token_ids, norm_gain=norm_gain, q_weight=q_weight, key_matrix=key_matrix, value_matrix=value_matrix, out_weight=out_weight, label_table=label_table, refresh_rows=refresh_rows, label_counts=label_counts, queries=queries, positives=positives)


rope_theta = 1000000.0
norm_eps = 1e-06
focal_beta = 0.9999

def rotary(values, head_size):
    length = values.shape[1]
    half = head_size // 2
    frequency = rope_theta ** (-2.0 * jnp.arange(half, dtype=jnp.float32) / head_size)
    angles = jnp.arange(length, dtype=jnp.float32)[:, None] * frequency[None, :]
    cosine = jnp.concatenate([jnp.cos(angles), jnp.cos(angles)], axis=1)[None, :, None, :]
    sine = jnp.concatenate([jnp.sin(angles), jnp.sin(angles)], axis=1)[None, :, None, :]
    turned = jnp.concatenate([-values[..., half:], values[..., :half]], axis=-1)
    return values * cosine + turned * sine

def attend(query_rows, key_rows, value_rows, text_ids, head_size):
    texts, length = text_ids.shape
    kv_heads = key_rows.shape[1] // head_size
    repeat = query_rows.shape[1] // head_size // kv_heads
    query_r = query_rows.astype(jnp.float32).reshape(texts, length, kv_heads, repeat, head_size)
    key_r = key_rows.astype(jnp.float32).reshape(texts, length, kv_heads, head_size)
    value_r = value_rows.astype(jnp.float32).reshape(texts, length, kv_heads, head_size)
    scores = jnp.einsum('ntgrd,nsgd->ngrts', query_r, key_r) / math.sqrt(head_size)
    causal = jnp.arange(length)[:, None] >= jnp.arange(length)[None, :]
    allowed = causal[None, None, None, :, :] & (text_ids != 0)[:, None, None, None, :]
    weights = jnp.where(allowed, jnp.exp(scores), 0.0)
    probs = (weights / lax.optimization_barrier(jnp.sum(weights, axis=-1, keepdims=True))).astype(jnp.bfloat16)
    mixed = jnp.einsum('ngrts,nsgd->ntgrd', probs.astype(jnp.float32), value_r)
    return mixed.reshape(texts * length, -1).astype(jnp.bfloat16)

def reference(hidden_states, token_ids, norm_gain, q_weight, key_matrix, value_matrix, out_weight, label_table, refresh_rows, label_counts, queries, positives):
    grouped = hidden_states.reshape(N_DP, LAB_GRP * TXT, MODEL_WIDTH)
    grouped_ids = token_ids.reshape(N_DP, LAB_GRP, TXT)

    def encode(pair):
        states = pair[0].astype(jnp.float32)
        text_ids = pair[1]
        scaled = lax.rsqrt(lax.optimization_barrier(jnp.mean(states * states, axis=1, keepdims=True)) + norm_eps)
        normed = (states * scaled * norm_gain).astype(jnp.bfloat16)
        query_raw = jnp.dot(normed, q_weight, preferred_element_type=jnp.float32)
        key_raw = jnp.dot(normed, key_matrix, preferred_element_type=jnp.float32)
        value_raw = jnp.dot(normed, value_matrix, preferred_element_type=jnp.float32)
        count_tokens = states.shape[0]
        queries_rot = rotary(query_raw.reshape(LAB_GRP, TXT, -1, HEAD_WIDTH), HEAD_WIDTH).reshape(count_tokens, -1).astype(jnp.bfloat16)
        rotary_keys = rotary(key_raw.reshape(LAB_GRP, TXT, -1, HEAD_WIDTH), HEAD_WIDTH).reshape(count_tokens, -1).astype(jnp.bfloat16)
        values_rot = value_raw.astype(jnp.bfloat16)
        attended = attend(queries_rot, rotary_keys, values_rot, text_ids, HEAD_WIDTH)
        projected = jnp.dot(attended, out_weight.T, preferred_element_type=jnp.float32)
        live = (text_ids != 0).astype(jnp.float32)
        summed = lax.optimization_barrier(jnp.sum((states + projected).reshape(LAB_GRP, TXT, MODEL_WIDTH) * live[:, :, None], axis=1))
        return (summed / lax.optimization_barrier(jnp.sum(live, axis=1, keepdims=True))).astype(jnp.bfloat16)
    refreshed = lax.map(encode, (grouped, grouped_ids)).reshape(TEXTS, MODEL_WIDTH)
    owners = jnp.arange(TEXTS, dtype=jnp.int32) // REF
    rows = (owners * LAB_OWN + refresh_rows).astype(jnp.int32)
    table = label_table.at[rows].set(refreshed)
    root = math.sqrt(MODEL_WIDTH)
    logits = jnp.dot(queries, table.T, preferred_element_type=jnp.float32) / root
    targets = jnp.zeros((BATCH, LABELS), jnp.float32).at[jnp.arange(BATCH, dtype=jnp.int32)[:, None], positives].set(1.0)
    signs = 2.0 * targets - 1.0
    margin = signs * logits
    balance = (1.0 - focal_beta) / -jnp.expm1(label_counts.astype(jnp.float32) * math.log(focal_beta))
    factor = LABELS / jnp.sum(balance)
    missed = jax.nn.sigmoid(-margin)
    softened = jax.nn.softplus(-margin)
    slopes = (balance[None, :] * signs * (-(missed * missed) * (2.0 * jax.nn.sigmoid(margin) * softened + missed))).astype(jnp.bfloat16)
    label_grad = factor * (jnp.dot(slopes.T, queries, preferred_element_type=jnp.float32) / root)
    query_grad = factor * (jnp.dot(slopes, table, preferred_element_type=jnp.float32) / root)
    loss = factor * jnp.sum(balance[None, :] * missed * missed * softened) / (BATCH * LABELS)
    return (label_grad, query_grad, loss)
```

```python
import math

import jax
import jax.numpy as jnp
from jax import lax
from jax.sharding import PartitionSpec as P

HEAD_WIDTH = 128


rope_theta = 1000000.0
norm_eps = 1e-06
focal_beta = 0.9999


def rotary(values, head_size):
    length = values.shape[1]
    half = head_size // 2
    frequency = rope_theta ** (-2.0 * jnp.arange(half, dtype=jnp.float32) / head_size)
    angles = jnp.arange(length, dtype=jnp.float32)[:, None] * frequency[None, :]
    cosine = jnp.concatenate([jnp.cos(angles), jnp.cos(angles)], axis=1)[None, :, None, :]
    sine = jnp.concatenate([jnp.sin(angles), jnp.sin(angles)], axis=1)[None, :, None, :]
    turned = jnp.concatenate([-values[..., half:], values[..., :half]], axis=-1)
    return values * cosine + turned * sine


def attend(query_rows, key_rows, value_rows, text_ids, head_size):
    texts, length = text_ids.shape
    kv_heads = key_rows.shape[1] // head_size
    repeat = query_rows.shape[1] // head_size // kv_heads
    query_r = query_rows.reshape(texts, length, kv_heads, repeat, head_size)
    key_r = key_rows.reshape(texts, length, kv_heads, head_size)
    value_r = value_rows.reshape(texts, length, kv_heads, head_size)
    scores = jnp.einsum(
        "ntgrd,nsgd->ngrts", query_r, key_r, preferred_element_type=jnp.float32
    ) / math.sqrt(head_size)
    causal = jnp.arange(length)[:, None] >= jnp.arange(length)[None, :]
    allowed = causal[None, None, None, :, :] & (text_ids != 0)[:, None, None, None, :]
    weights = jnp.where(allowed, jnp.exp(scores), 0.0)
    probs = (weights / jnp.sum(weights, axis=-1, keepdims=True)).astype(jnp.bfloat16)
    mixed = jnp.einsum("ngrts,nsgd->ntgrd", probs, value_r, preferred_element_type=jnp.float32)
    return mixed.reshape(texts * length, -1).astype(jnp.bfloat16)


def shards(
    hidden_states,
    token_ids,
    norm_gain,
    q_weight,
    key_matrix,
    value_matrix,
    out_weight,
    label_table,
    refresh_rows,
    label_counts,
    queries,
    positives,
):
    width = hidden_states.shape[1]
    group_tokens = hidden_states.shape[0]
    texts, length = token_ids.shape
    states = hidden_states.astype(jnp.float32)
    scaled = lax.rsqrt(jnp.mean(states * states, axis=1, keepdims=True) + norm_eps)
    normed = (states * scaled * norm_gain).astype(jnp.bfloat16)
    heads = q_weight.shape[1]
    kv = key_matrix.shape[1]
    weights = lax.all_gather(
        jnp.concatenate([q_weight, key_matrix, value_matrix], axis=1), "dp", axis=0, tiled=True
    )
    raw = jnp.dot(normed, weights, preferred_element_type=jnp.float32)
    query_raw = raw[:, :heads]
    key_raw = raw[:, heads : heads + kv]
    value_raw = raw[:, heads + kv :]
    queries_rot = (
        rotary(query_raw.reshape(texts, length, -1, HEAD_WIDTH), HEAD_WIDTH)
        .reshape(group_tokens, -1)
        .astype(jnp.bfloat16)
    )
    rotary_keys = (
        rotary(key_raw.reshape(texts, length, -1, HEAD_WIDTH), HEAD_WIDTH)
        .reshape(group_tokens, -1)
        .astype(jnp.bfloat16)
    )
    values_rot = value_raw.astype(jnp.bfloat16)
    attended = attend(queries_rot, rotary_keys, values_rot, token_ids, HEAD_WIDTH)
    live = (token_ids != 0).astype(jnp.float32)
    counted = jnp.sum(live, axis=1, keepdims=True)
    pooled = (
        jnp.sum(attended.astype(jnp.float32).reshape(texts, length, -1) * live[:, :, None], axis=1)
        / counted
    ).astype(jnp.bfloat16)
    groups = lax.axis_size("dp")
    members = lax.axis_size("mp")
    share = texts // members
    member = lax.axis_index("mp")
    live_own = lax.dynamic_slice_in_dim(live, member * share, share, 0)
    states_own = lax.dynamic_slice_in_dim(
        hidden_states, member * share * length, share * length, 0
    ).reshape(share, length, width)
    counted_own = jnp.sum(live_own, axis=1, keepdims=True)
    base_own = (
        jnp.sum(states_own.astype(jnp.float32) * live_own[:, :, None], axis=1) / counted_own
    )
    pooled_all = lax.all_gather(pooled, "dp", axis=0, tiled=True)
    terms = lax.dot_general(
        pooled_all, out_weight, (((1,), (1,)), ((), ())), preferred_element_type=jnp.float32
    ).reshape(groups, members, share, -1)
    mine = lax.psum_scatter(terms, "mp", scatter_dimension=1, tiled=True)
    mine = mine.reshape(groups, share, -1)
    swapped = lax.all_to_all(mine, "dp", 0, 0, tiled=True)
    projected = jnp.swapaxes(swapped, 0, 1).reshape(share, width)
    refreshed = (base_own + projected).astype(jnp.bfloat16)

    root = math.sqrt(width)
    owned = label_table.shape[0]
    first_label = (lax.axis_index("dp") * members + member) * owned
    label_ids = first_label + jnp.arange(owned, dtype=jnp.int32)
    balance = balances(label_counts)
    replaced = jnp.any(
        refresh_rows[:, None] == jnp.arange(owned, dtype=jnp.int32)[None, :], axis=0
    )
    kept = jnp.where(replaced, 0.0, balance)
    early_slopes, early_loss = focal(queries, label_table, positives, label_ids, kept, root)
    query_part = jnp.dot(early_slopes, label_table, preferred_element_type=jnp.float32) / root
    query_sum, loss_sum, summed_weight = lax.psum(
        (query_part, early_loss, jnp.sum(balance)), ("dp", "mp")
    )
    new_ids = lax.all_gather(first_label + refresh_rows, ("dp", "mp"), axis=0, tiled=True)
    new_balance = lax.all_gather(balance[refresh_rows], ("dp", "mp"), axis=0, tiled=True)
    refreshed_all = lax.all_gather(refreshed, ("dp", "mp"), axis=0, tiled=True)
    late_slopes, late_loss = focal(queries, refreshed_all, positives, new_ids, new_balance, root)
    query_late = jnp.dot(late_slopes, refreshed_all, preferred_element_type=jnp.float32) / root
    own_late = lax.dynamic_slice_in_dim(
        late_slopes, (lax.axis_index("dp") * members + member) * share, share, 1
    )
    slopes = early_slopes.at[:, refresh_rows].set(own_late)
    label_part = (
        lax.dot_general(
            slopes, queries, (((0,), (0,)), ((), ())), preferred_element_type=jnp.float32
        )
        / root
    )
    total_labels = owned * groups * members
    factor = total_labels / summed_weight
    loss = factor * (loss_sum + late_loss) / (queries.shape[0] * total_labels)
    return (factor * label_part, factor * (query_sum + query_late), loss)


def balances(label_counts):
    return (1.0 - focal_beta) / -jnp.expm1(
        label_counts.astype(jnp.float32) * math.log(focal_beta)
    )


def focal(queries, table, positives, label_ids, balance, root):
    logits = (
        lax.dot_general(
            queries, table, (((1,), (1,)), ((), ())), preferred_element_type=jnp.float32
        )
        / root
    )
    matched = jnp.any(positives[:, :, None] == label_ids[None, None, :], axis=1)
    signs = jnp.where(matched, 1.0, -1.0)
    margin = signs * logits
    missed = jax.nn.sigmoid(-margin)
    softened = jax.nn.softplus(-margin)
    loss = jnp.sum(balance[None, :] * missed * missed * softened)
    slopes = (
        balance[None, :]
        * signs
        * (-(missed * missed) * (2.0 * jax.nn.sigmoid(margin) * softened + missed))
    ).astype(jnp.bfloat16)
    return slopes, loss


def solution(mesh):
    in_specs = (
        P("dp", None),
        P("dp", None),
        P(),
        P("dp", "mp"),
        P("dp", "mp"),
        P("dp", "mp"),
        P("dp", "mp"),
        P(("dp", "mp"), None),
        P(("dp", "mp")),
        P(("dp", "mp")),
        P(),
        P(),
    )
    out_specs = (P(("dp", "mp"), None), P(), P())
    return jax.shard_map(shards, mesh=mesh, in_specs=in_specs, out_specs=out_specs, check_vma=False)
```

```python
import functools
import math

import jax
import jax.numpy as jnp
from jax import lax
from jax.experimental import pallas as pl
from jax.experimental.pallas import tpu as pltpu
from jax.sharding import PartitionSpec as P

MESH = pl.DeviceIdType.MESH

HEAD_WIDTH = 128


rope_theta = 1000000.0
norm_eps = 1e-06
focal_beta = 0.9999


def rotary(values, head_size):
    length = values.shape[1]
    half = head_size // 2
    frequency = rope_theta ** (-2.0 * jnp.arange(half, dtype=jnp.float32) / head_size)
    angles = jnp.arange(length, dtype=jnp.float32)[:, None] * frequency[None, :]
    cosine = jnp.concatenate([jnp.cos(angles), jnp.cos(angles)], axis=1)[None, :, None, :]
    sine = jnp.concatenate([jnp.sin(angles), jnp.sin(angles)], axis=1)[None, :, None, :]
    turned = jnp.concatenate([-values[..., half:], values[..., :half]], axis=-1)
    return values * cosine + turned * sine


def attend(query_rows, key_rows, value_rows, text_ids, head_size):
    texts, length = text_ids.shape
    kv_heads = key_rows.shape[1] // head_size
    repeat = query_rows.shape[1] // head_size // kv_heads
    query_r = query_rows.reshape(texts, length, kv_heads, repeat, head_size)
    key_r = key_rows.reshape(texts, length, kv_heads, head_size)
    value_r = value_rows.reshape(texts, length, kv_heads, head_size)
    scores = jnp.einsum(
        "ntgrd,nsgd->ngrts", query_r, key_r, preferred_element_type=jnp.float32
    ) / math.sqrt(head_size)
    causal = jnp.arange(length)[:, None] >= jnp.arange(length)[None, :]
    allowed = causal[None, None, None, :, :] & (text_ids != 0)[:, None, None, None, :]
    weights = jnp.where(allowed, jnp.exp(scores), 0.0)
    probs = (weights / jnp.sum(weights, axis=-1, keepdims=True)).astype(jnp.bfloat16)
    mixed = jnp.einsum("ngrts,nsgd->ntgrd", probs, value_r, preferred_element_type=jnp.float32)
    return mixed.reshape(texts * length, -1).astype(jnp.bfloat16)


def remote(source, target, send, receive, device):
    return pltpu.make_async_remote_copy(
        src_ref=source,
        dst_ref=target,
        send_sem=send,
        recv_sem=receive,
        device_id=device,
        device_id_type=MESH,
    )


def each(low, high, body):
    def run(index, carry):
        body(index)
        return carry

    lax.fori_loop(low, high, run, 0)


def spread(groups, members, blocks, group_sem, far_sem, core_sem, relay_sem, arrived):
    group, member = lax.axis_index("dp"), lax.axis_index("mp")
    far = lax.rem(member + 2, members)
    core = member + 1 - 2 * lax.rem(member, 2)
    far_core = lax.rem(core + 2, members)

    def copy(at, slot, sems, index, device):
        return remote(blocks.at[slot], blocks.at[slot], sems.at[index], arrived.at[slot], device)

    def forward(at):
        slot = at * members + member
        copy(at, slot, far_sem, at, (group, far)).start()
        copy(at, slot, core_sem, at, (group, core)).start()

    def send(step):
        slot = group * members + member
        copy(group, slot, group_sem, step, (lax.rem(group + step, groups), member)).start()

    def pass_on(step):
        at = lax.rem(group + groups - step, groups)
        slot = at * members + member
        copy(at, slot, group_sem, step, (at, member)).wait_recv()
        forward(at)

    def relay(step):
        at = lax.rem(group + groups - step, groups)
        slot = at * members + far
        copy(at, slot, far_sem, at, (group, far)).wait_recv()
        copy(at, slot, relay_sem, at, (group, core)).start()

    def finish(at):
        copy(at, at * members + core, core_sem, at, (group, core)).wait_recv()
        copy(at, at * members + far_core, relay_sem, at, (group, core)).wait_recv()
        copy(at, at * members + member, far_sem, at, (group, far)).wait_send()
        copy(at, at * members + member, core_sem, at, (group, core)).wait_send()
        copy(at, at * members + far, relay_sem, at, (group, core)).wait_send()

    def sent(step):
        slot = group * members + member
        copy(group, slot, group_sem, step, (lax.rem(group + step, groups), member)).wait_send()

    each(1, groups, send)
    forward(group)
    each(1, groups, pass_on)
    each(0, groups, relay)
    each(0, groups, finish)
    each(1, groups, sent)


def spread_sems(groups, members):
    return [
        pltpu.SemaphoreType.DMA((groups,)),
        pltpu.SemaphoreType.DMA((groups,)),
        pltpu.SemaphoreType.DMA((groups,)),
        pltpu.SemaphoreType.DMA((groups,)),
        pltpu.SemaphoreType.DMA((groups * members,)),
    ]


def early_kernel(
    groups, members, part, meta, blocks, got, sums, terms, s1, r1, s2, r2, *sems
):
    group, member = lax.axis_index("dp"), lax.axis_index("mp")
    own = group * members + member
    rows = part.shape[1] // members
    barrier = pltpu.get_barrier_semaphore()

    def greet_member(step):
        peer = lax.rem(member + step, members)
        pl.semaphore_signal(barrier, inc=1, device_id=(group, peer), device_id_type=MESH)

    def greet_group(step):
        peer = lax.rem(group + step, groups)
        pl.semaphore_signal(barrier, inc=1, device_id=(peer, member), device_id_type=MESH)

    each(1, members, greet_member)
    each(1, groups, greet_group)
    pl.semaphore_wait(barrier, groups + members - 2)

    def member_copy(step):
        peer = lax.rem(member + step, members)
        start = pl.multiple_of(peer * rows, rows)
        return remote(
            part.at[:, pl.ds(start, rows), :],
            got.at[member],
            s1.at[step],
            r1.at[member],
            (group, peer),
        )

    def member_wait(step):
        source = lax.rem(member + members - step, members)
        remote(
            got.at[source], got.at[source], s1.at[step], r1.at[source], (group, source)
        ).wait_recv()

    each(1, members, lambda step: member_copy(step).start())
    each(1, members, member_wait)
    first = pl.multiple_of(member * rows, rows)

    def add_members(at):
        total = part[at, pl.ds(first, rows), :]
        for step in range(1, members):
            total = total + got[lax.rem(member + step, members), at]
        sums[at] = total

    each(0, groups, add_members)

    def group_copy(step):
        peer = lax.rem(group + step, groups)
        return remote(sums.at[peer], terms.at[group], s2.at[step], r2.at[group], (peer, member))

    def group_wait(step):
        source = lax.rem(group + groups - step, groups)
        remote(
            terms.at[source], terms.at[source], s2.at[step], r2.at[source], (source, member)
        ).wait_recv()

    each(1, groups, lambda step: group_copy(step).start())
    each(1, groups, group_wait)
    total = sums[group]
    for step in range(1, groups):
        total = total + terms[lax.rem(group + step, groups)]
    blocks[own, :rows] = total
    blocks[own, rows:] = meta[...]
    spread(groups, members, blocks, *sems)
    each(1, members, lambda step: member_copy(step).wait_send())
    each(1, groups, lambda step: group_copy(step).wait_send())


def early_reduce(part, meta, groups, members):
    _, batch, block = part.shape
    rows = batch // members
    return pl.pallas_call(
        functools.partial(early_kernel, groups, members),
        out_shape=jax.ShapeDtypeStruct(
            (groups * members, rows + meta.shape[0], block), jnp.float32
        ),
        in_specs=[pl.BlockSpec(memory_space=pltpu.VMEM)] * 2,
        out_specs=pl.BlockSpec(memory_space=pltpu.VMEM),
        scratch_shapes=[
            pltpu.VMEM((members, groups, rows, block), jnp.float32),
            pltpu.VMEM((groups, rows, block), jnp.float32),
            pltpu.VMEM((groups, rows, block), jnp.float32),
            pltpu.SemaphoreType.DMA((members,)),
            pltpu.SemaphoreType.DMA((members,)),
            pltpu.SemaphoreType.DMA((groups,)),
            pltpu.SemaphoreType.DMA((groups,)),
            *spread_sems(groups, members),
        ],
        compiler_params=pltpu.CompilerParams(
            collective_id=0, has_side_effects=True, vmem_limit_bytes=24 << 20
        ),
        name="early_reduce",
    )(part, meta)


def tail_kernel(
    groups, members, pooled, weight, base, blocks, pool, terms, parts, s1, r1, s2, r2, *sems
):
    group, member = lax.axis_index("dp"), lax.axis_index("mp")
    own = group * members + member
    devices = groups * members
    share = terms.shape[1]
    barrier = pltpu.get_barrier_semaphore()

    def greet(step):
        peer = lax.rem(own + step, devices)
        pl.semaphore_signal(
            barrier,
            inc=1,
            device_id=(peer // members, lax.rem(peer, members)),
            device_id_type=MESH,
        )

    each(1, devices, greet)
    pl.semaphore_wait(barrier, devices - 1)

    def pool_copy(step):
        peer = lax.rem(group + step, groups)
        return remote(pooled, pool.at[group], s1.at[step], r1.at[group], (peer, member))

    def part_copy(owner_group, owner_member):
        slot = owner_group * members + owner_member
        return remote(
            terms.at[slot], parts.at[own], s2.at[slot], r2.at[own], (owner_group, owner_member)
        )

    def product(at, rows):
        made = jnp.dot(rows, weight[...], preferred_element_type=jnp.float32)
        for index in range(members):
            terms[at * members + index] = made[index * share : (index + 1) * share]

    def project(step):
        at = lax.rem(group + groups - step, groups)
        remote(pooled, pool.at[at], s1.at[step], r1.at[at], (at, member)).wait_recv()
        product(at, pool[at])
        each(0, members, lambda index: part_copy(at, index).start())

    each(1, groups, lambda step: pool_copy(step).start())
    product(group, pooled[...])
    each(1, members, lambda step: part_copy(group, lax.rem(member + step, members)).start())
    parts[own] = terms[own]
    each(1, groups, project)

    def part_wait(step):
        source = lax.rem(own + devices - step, devices)
        remote(
            terms.at[source],
            parts.at[source],
            s2.at[source],
            r2.at[source],
            (source // members, lax.rem(source, members)),
        ).wait_recv()

    each(1, devices, part_wait)
    rows = []
    for at in range(groups):
        total = base[at]
        for index in range(members):
            total = total + parts[at * members + index]
        rows.append(total)
    blocks[own] = jnp.concatenate(rows, axis=0).astype(jnp.bfloat16)
    spread(groups, members, blocks, *sems)
    each(1, groups, lambda step: pool_copy(step).wait_send())

    def part_sent(step):
        slot = lax.rem(own + step, devices)
        part_copy(slot // members, lax.rem(slot, members)).wait_send()

    each(1, devices, part_sent)


def tail(pooled, weight, base, groups, members):
    texts, heads = pooled.shape
    block = weight.shape[1]
    share = texts // members
    devices = groups * members
    return pl.pallas_call(
        functools.partial(tail_kernel, groups, members),
        out_shape=jax.ShapeDtypeStruct((devices, groups * share, block), jnp.bfloat16),
        in_specs=[pl.BlockSpec(memory_space=pltpu.VMEM)] * 3,
        out_specs=pl.BlockSpec(memory_space=pltpu.VMEM),
        scratch_shapes=[
            pltpu.VMEM((groups, texts, heads), jnp.bfloat16),
            pltpu.VMEM((devices, share, block), jnp.float32),
            pltpu.VMEM((devices, share, block), jnp.float32),
            pltpu.SemaphoreType.DMA((groups,)),
            pltpu.SemaphoreType.DMA((groups,)),
            pltpu.SemaphoreType.DMA((devices,)),
            pltpu.SemaphoreType.DMA((devices,)),
            *spread_sems(groups, members),
        ],
        compiler_params=pltpu.CompilerParams(
            collective_id=1, has_side_effects=True, vmem_limit_bytes=24 << 20
        ),
        name="tail",
    )(pooled, weight, base)


def kernels_fit(groups, members, width, share):
    lanes = -(-(width // groups) // 128) * 128
    return members == 4 and groups * members * groups * share * lanes * 2 < 8 << 20


def shards(
    hidden_states,
    token_ids,
    norm_gain,
    q_weight,
    key_matrix,
    value_matrix,
    out_weight,
    label_table,
    refresh_rows,
    label_counts,
    queries,
    positives,
):
    width = hidden_states.shape[1]
    group_tokens = hidden_states.shape[0]
    texts, length = token_ids.shape
    states = hidden_states.astype(jnp.float32)
    scaled = lax.rsqrt(jnp.mean(states * states, axis=1, keepdims=True) + norm_eps)
    normed = (states * scaled * norm_gain).astype(jnp.bfloat16)
    heads = q_weight.shape[1]
    kv = key_matrix.shape[1]
    weights = lax.all_gather(
        jnp.concatenate([q_weight, key_matrix, value_matrix], axis=1), "dp", axis=0, tiled=True
    )
    raw = jnp.dot(normed, weights, preferred_element_type=jnp.float32)
    query_raw = raw[:, :heads]
    key_raw = raw[:, heads : heads + kv]
    value_raw = raw[:, heads + kv :]
    queries_rot = (
        rotary(query_raw.reshape(texts, length, -1, HEAD_WIDTH), HEAD_WIDTH)
        .reshape(group_tokens, -1)
        .astype(jnp.bfloat16)
    )
    rotary_keys = (
        rotary(key_raw.reshape(texts, length, -1, HEAD_WIDTH), HEAD_WIDTH)
        .reshape(group_tokens, -1)
        .astype(jnp.bfloat16)
    )
    values_rot = value_raw.astype(jnp.bfloat16)
    attended = attend(queries_rot, rotary_keys, values_rot, token_ids, HEAD_WIDTH)
    live = (token_ids != 0).astype(jnp.float32)
    counted = jnp.sum(live, axis=1, keepdims=True)
    pooled = (
        jnp.sum(attended.astype(jnp.float32).reshape(texts, length, -1) * live[:, :, None], axis=1)
        / counted
    ).astype(jnp.bfloat16)
    groups = lax.axis_size("dp")
    members = lax.axis_size("mp")
    share = texts // members
    member = lax.axis_index("mp")
    live_own = lax.dynamic_slice_in_dim(live, member * share, share, 0)
    states_own = lax.dynamic_slice_in_dim(
        hidden_states, member * share * length, share * length, 0
    ).reshape(share, length, width)
    counted_own = jnp.sum(live_own, axis=1, keepdims=True)
    base_own = (
        jnp.sum(states_own.astype(jnp.float32) * live_own[:, :, None], axis=1) / counted_own
    )
    block = width // groups
    use_kernels = kernels_fit(groups, members, width, share)
    if use_kernels:
        base_blocks = jnp.swapaxes(base_own.reshape(share, groups, block), 0, 1)
        gathered = tail(pooled, out_weight.T, base_blocks, groups, members)
        refreshed_all = jnp.swapaxes(
            gathered.reshape(groups * members, groups, share, block), 1, 2
        ).reshape(groups * members * share, width)
    else:
        refreshed_all = gather_refreshed(pooled, out_weight, base_own, groups, members)

    root = math.sqrt(width)
    owned = label_table.shape[0]
    first_label = (lax.axis_index("dp") * members + member) * owned
    label_ids = first_label + jnp.arange(owned, dtype=jnp.int32)
    balance = balances(label_counts)
    replaced = jnp.any(
        refresh_rows[:, None] == jnp.arange(owned, dtype=jnp.int32)[None, :], axis=0
    )
    kept = jnp.where(replaced, 0.0, balance)
    early_slopes, early_loss = focal(queries, label_table, positives, label_ids, kept, root)
    new_ids = first_label + refresh_rows
    if use_kernels:
        part = jnp.swapaxes(
            (jnp.dot(early_slopes, label_table, preferred_element_type=jnp.float32) / root).reshape(
                queries.shape[0], groups, block
            ),
            0,
            1,
        )
        scalars = jnp.stack([early_loss, jnp.sum(balance)] + [jnp.float32(0)] * (share - 2))
        meta = jnp.pad(
            jnp.stack([new_ids.astype(jnp.float32), balance[refresh_rows], scalars]),
            ((0, 5), (0, block - share)),
        )
        reduced = early_reduce(part, meta, groups, members)
        rows = queries.shape[0] // members
        query_sum = (
            reduced[:, :rows]
            .reshape(groups, members, rows, block)
            .transpose(1, 2, 0, 3)
            .reshape(queries.shape[0], width)
        )
        new_ids = reduced[:, rows, :share].reshape(-1).astype(jnp.int32)
        new_balance = reduced[:, rows + 1, :share].reshape(-1)
        loss_sum = jnp.sum(reduced[:, rows + 2, 0])
        summed_weight = jnp.sum(reduced[:, rows + 2, 1])
    else:
        query_part = jnp.dot(early_slopes, label_table, preferred_element_type=jnp.float32) / root
        query_sum, loss_sum, summed_weight = lax.psum(
            (query_part, early_loss, jnp.sum(balance)), ("dp", "mp")
        )
        new_ids = lax.all_gather(new_ids, ("dp", "mp"), axis=0, tiled=True)
        new_balance = lax.all_gather(balance[refresh_rows], ("dp", "mp"), axis=0, tiled=True)
    late_slopes, late_loss = focal(queries, refreshed_all, positives, new_ids, new_balance, root)
    query_late = jnp.dot(late_slopes, refreshed_all, preferred_element_type=jnp.float32) / root
    own_late = lax.dynamic_slice_in_dim(
        late_slopes, (lax.axis_index("dp") * members + member) * share, share, 1
    )
    slopes = early_slopes.at[:, refresh_rows].set(own_late)
    label_part = (
        lax.dot_general(
            slopes, queries, (((0,), (0,)), ((), ())), preferred_element_type=jnp.float32
        )
        / root
    )
    total_labels = owned * groups * members
    factor = total_labels / summed_weight
    loss = factor * (loss_sum + late_loss) / (queries.shape[0] * total_labels)
    return (factor * label_part, factor * (query_sum + query_late), loss)


def gather_refreshed(pooled, out_weight, base_own, groups, members):
    share, width = base_own.shape
    pooled_all = lax.all_gather(pooled, "dp", axis=0, tiled=True)
    terms = lax.dot_general(
        pooled_all, out_weight, (((1,), (1,)), ((), ())), preferred_element_type=jnp.float32
    ).reshape(groups, members, share, -1)
    mine = lax.psum_scatter(terms, "mp", scatter_dimension=1, tiled=True)
    swapped = lax.all_to_all(mine.reshape(groups, share, -1), "dp", 0, 0, tiled=True)
    projected = jnp.swapaxes(swapped, 0, 1).reshape(share, width)
    refreshed = (base_own + projected).astype(jnp.bfloat16)
    return lax.all_gather(refreshed, ("dp", "mp"), axis=0, tiled=True)


def balances(label_counts):
    return (1.0 - focal_beta) / -jnp.expm1(
        label_counts.astype(jnp.float32) * math.log(focal_beta)
    )


def focal(queries, table, positives, label_ids, balance, root):
    logits = (
        lax.dot_general(
            queries, table, (((1,), (1,)), ((), ())), preferred_element_type=jnp.float32
        )
        / root
    )
    matched = jnp.any(positives[:, :, None] == label_ids[None, None, :], axis=1)
    signs = jnp.where(matched, 1.0, -1.0)
    margin = signs * logits
    missed = jax.nn.sigmoid(-margin)
    softened = jax.nn.softplus(-margin)
    loss = jnp.sum(balance[None, :] * missed * missed * softened)
    slopes = (
        balance[None, :]
        * signs
        * (-(missed * missed) * (2.0 * jax.nn.sigmoid(margin) * softened + missed))
    ).astype(jnp.bfloat16)
    return slopes, loss


def solution(mesh):
    in_specs = (
        P("dp", None),
        P("dp", None),
        P(),
        P("dp", "mp"),
        P("dp", "mp"),
        P("dp", "mp"),
        P("dp", "mp"),
        P(("dp", "mp"), None),
        P(("dp", "mp")),
        P(("dp", "mp")),
        P(),
        P(),
    )
    out_specs = (P(("dp", "mp"), None), P(), P())
    return jax.shard_map(shards, mesh=mesh, in_specs=in_specs, out_specs=out_specs, check_vma=False)
```

```python
import functools
import math

import jax
import jax.numpy as jnp
from jax import lax
from jax.experimental import pallas as pl
from jax.experimental.pallas import tpu as pltpu
from jax.sharding import PartitionSpec as P

MESH = pl.DeviceIdType.MESH
SIDES = 2

HEAD_WIDTH = 128


rope_theta = 1000000.0
norm_eps = 1e-06
focal_beta = 0.9999


def rotary(values, head_size):
    length = values.shape[1]
    half = head_size // 2
    frequency = rope_theta ** (-2.0 * jnp.arange(half, dtype=jnp.float32) / head_size)
    angles = jnp.arange(length, dtype=jnp.float32)[:, None] * frequency[None, :]
    cosine = jnp.concatenate([jnp.cos(angles), jnp.cos(angles)], axis=1)[None, :, None, :]
    sine = jnp.concatenate([jnp.sin(angles), jnp.sin(angles)], axis=1)[None, :, None, :]
    turned = jnp.concatenate([-values[..., half:], values[..., :half]], axis=-1)
    return values * cosine + turned * sine


def attend(query_rows, key_rows, value_rows, text_ids, head_size):
    texts, length = text_ids.shape
    kv_heads = key_rows.shape[1] // head_size
    repeat = query_rows.shape[1] // head_size // kv_heads
    query_r = query_rows.reshape(texts, length, kv_heads, repeat, head_size)
    key_r = key_rows.reshape(texts, length, kv_heads, head_size)
    value_r = value_rows.reshape(texts, length, kv_heads, head_size)
    scores = jnp.einsum(
        "ntgrd,nsgd->ngrts", query_r, key_r, preferred_element_type=jnp.float32
    ) / math.sqrt(head_size)
    causal = jnp.arange(length)[:, None] >= jnp.arange(length)[None, :]
    allowed = causal[None, None, None, :, :] & (text_ids != 0)[:, None, None, None, :]
    weights = jnp.where(allowed, jnp.exp(scores), 0.0)
    probs = (weights / jnp.sum(weights, axis=-1, keepdims=True)).astype(jnp.bfloat16)
    mixed = jnp.einsum("ngrts,nsgd->ntgrd", probs, value_r, preferred_element_type=jnp.float32)
    return mixed.reshape(texts * length, -1).astype(jnp.bfloat16)


def remote(source, target, send, receive, device):
    return pltpu.make_async_remote_copy(
        src_ref=source,
        dst_ref=target,
        send_sem=send,
        recv_sem=receive,
        device_id=device,
        device_id_type=MESH,
    )


def each(low, high, body):
    def run(index, carry):
        body(index)
        return carry

    lax.fori_loop(low, high, run, 0)


def spread(groups, members, blocks, group_sem, far_sem, core_sem, relay_sem, arrived):
    group, member = lax.axis_index("dp"), lax.axis_index("mp")
    far = lax.rem(member + 2, members)
    core = member + 1 - 2 * lax.rem(member, 2)
    far_core = lax.rem(core + 2, members)

    def copy(at, slot, sems, index, device):
        return remote(blocks.at[slot], blocks.at[slot], sems.at[index], arrived.at[slot], device)

    def forward(at):
        slot = at * members + member
        copy(at, slot, far_sem, at, (group, far)).start()
        copy(at, slot, core_sem, at, (group, core)).start()

    def send(step):
        slot = group * members + member
        copy(group, slot, group_sem, step, (lax.rem(group + step, groups), member)).start()

    def pass_on(step):
        at = lax.rem(group + groups - step, groups)
        slot = at * members + member
        copy(at, slot, group_sem, step, (at, member)).wait_recv()
        forward(at)

    def relay(step):
        at = lax.rem(group + groups - step, groups)
        slot = at * members + far
        copy(at, slot, far_sem, at, (group, far)).wait_recv()
        copy(at, slot, relay_sem, at, (group, core)).start()

    def finish(at):
        copy(at, at * members + core, core_sem, at, (group, core)).wait_recv()
        copy(at, at * members + far_core, relay_sem, at, (group, core)).wait_recv()
        copy(at, at * members + member, far_sem, at, (group, far)).wait_send()
        copy(at, at * members + member, core_sem, at, (group, core)).wait_send()
        copy(at, at * members + far, relay_sem, at, (group, core)).wait_send()

    def sent(step):
        slot = group * members + member
        copy(group, slot, group_sem, step, (lax.rem(group + step, groups), member)).wait_send()

    def start():
        each(1, groups, send)
        forward(group)

    def end():
        each(1, groups, pass_on)
        each(0, groups, relay)
        each(0, groups, finish)
        each(1, groups, sent)

    return start, end


def spread_sems(groups, members):
    return [
        pltpu.SemaphoreType.DMA((groups,)),
        pltpu.SemaphoreType.DMA((groups,)),
        pltpu.SemaphoreType.DMA((groups,)),
        pltpu.SemaphoreType.DMA((groups,)),
        pltpu.SemaphoreType.DMA((groups * members,)),
    ]


def project_kernel(
    groups,
    members,
    states,
    gain,
    q_weight,
    key_matrix,
    value_matrix,
    queries,
    table,
    positives,
    label_ids,
    kept,
    meta,
    raw,
    slopes,
    blocks,
    weights,
    normed,
    part,
    got,
    sums,
    terms,
    up_sem,
    down_sem,
    side_sem,
    landed,
    s1,
    r1,
    s2,
    r2,
    *sems,
):
    group, member = lax.axis_index("dp"), lax.axis_index("mp")
    own = group * members + member
    depth = groups // SIDES
    level, side = group // SIDES, lax.rem(group, SIDES)
    block = table.shape[1] // groups
    rows = queries.shape[0] // members
    heads, kv = q_weight.shape[1], key_matrix.shape[1]
    barrier = pltpu.get_barrier_semaphore()

    def greet_member(step):
        peer = lax.rem(member + step, members)
        pl.semaphore_signal(barrier, inc=1, device_id=(group, peer), device_id_type=MESH)

    def greet_group(step):
        peer = lax.rem(group + step, groups)
        pl.semaphore_signal(barrier, inc=1, device_id=(peer, member), device_id_type=MESH)

    each(1, members, greet_member)
    each(1, groups, greet_group)
    weights[group, :, :heads] = q_weight[...]
    weights[group, :, heads : heads + kv] = key_matrix[...]
    weights[group, :, heads + kv :] = value_matrix[...]
    pl.semaphore_wait(barrier, groups + members - 2)

    def weight_copy(slot, sem, peer):
        return remote(
            weights.at[slot], weights.at[slot], sem.at[slot], landed.at[slot], (peer, member)
        )

    def up(slot):
        return weight_copy(slot, up_sem, group + SIDES)

    def down(slot):
        return weight_copy(slot, down_sem, group - SIDES)

    def across(slot):
        return weight_copy(slot, side_sem, level * SIDES + 1 - side)

    def travel(step):
        @pl.when(level >= step)
        def _():
            slot = group - step * SIDES
            if step > 0:
                weight_copy(slot, down_sem, group - SIDES).wait_recv()

            @pl.when(level < depth - 1)
            def _():
                up(slot).start()

            across(slot).start()

        if step == 0:

            @pl.when(level > 0)
            def _():
                down(group).start()

        else:

            @pl.when(level + step < depth)
            def _():
                slot = group + step * SIDES
                weight_copy(slot, up_sem, group + SIDES).wait_recv()

                @pl.when(level > 0)
                def _():
                    down(slot).start()

                across(slot).start()

    tokens = states.shape[0]
    tile = 128 if tokens % 128 == 0 else tokens

    def multiply(slot):
        def some(index):
            at = pl.ds(pl.multiple_of(index * tile, tile), tile)
            raw[at, :] += jnp.dot(
                normed[slot, at, :], weights[slot], preferred_element_type=jnp.float32
            )

        each(0, tokens // tile, some)

    def multiply_step(step):
        @pl.when(level >= step)
        def _():
            multiply(group - step * SIDES)

        if step > 0:

            @pl.when(level + step < depth)
            def _():
                multiply(group + step * SIDES)

    def multiply_across(step):
        def one(at):
            slot = at * SIDES + 1 - side
            across(slot).wait_recv()
            multiply(slot)

        @pl.when(level >= step)
        def _():
            one(level - step)

        if step > 0:

            @pl.when(level + step < depth)
            def _():
                one(level + step)

    travel(0)

    root = math.sqrt(table.shape[1])
    logits = (
        lax.dot_general(
            queries[...],
            table[...],
            (((1,), (1,)), ((), ())),
            preferred_element_type=jnp.float32,
        )
        / root
    )
    matched = positives[:, 0:1] == label_ids[...]
    for index in range(1, positives.shape[1]):
        matched = matched | (positives[:, index : index + 1] == label_ids[...])
    signs = jnp.where(matched, 1.0, -1.0)
    margin = signs * logits
    small = jnp.exp(-jnp.abs(margin))
    larger, smaller = 1.0 / (1.0 + small), small / (1.0 + small)
    missed = jnp.where(margin >= 0.0, smaller, larger)
    hit = jnp.where(margin >= 0.0, larger, smaller)
    softened = jnp.maximum(-margin, 0.0) + jnp.log1p(small)
    loss = jnp.sum(kept[...] * missed * missed * softened)
    early = (
        kept[...] * signs * (-(missed * missed) * (2.0 * hit * softened + missed))
    ).astype(jnp.bfloat16)
    slopes[...] = early
    for at in range(groups):
        part[at] = (
            jnp.dot(
                early,
                table[:, at * block : (at + 1) * block],
                preferred_element_type=jnp.float32,
            )
            / root
        )

    def member_copy(step):
        peer = lax.rem(member + step, members)
        start = pl.multiple_of(peer * rows, rows)
        return remote(
            part.at[:, pl.ds(start, rows), :],
            got.at[member],
            s1.at[step],
            r1.at[member],
            (group, peer),
        )

    def member_wait(step):
        source = lax.rem(member + members - step, members)
        remote(
            got.at[source], got.at[source], s1.at[step], r1.at[source], (group, source)
        ).wait_recv()

    each(1, members, lambda step: member_copy(step).start())

    def normalize(index):
        at = pl.ds(pl.multiple_of(index * 64, 64), 64)
        wide = states[at, :].astype(jnp.float32)
        scaled = lax.rsqrt(jnp.mean(wide * wide, axis=1, keepdims=True) + norm_eps)
        ready = (wide * scaled * gain[...]).astype(jnp.bfloat16)
        for piece in range(groups):
            normed[piece, at, :] = ready[:, piece * block : (piece + 1) * block]

    each(0, tokens // 64, normalize)
    raw[...] = jnp.zeros_like(raw)
    multiply_step(0)
    travel(1)
    each(1, members, member_wait)
    first = pl.multiple_of(member * rows, rows)

    def add_members(at):
        total = part[at, pl.ds(first, rows), :]
        for step in range(1, members):
            total = total + got[lax.rem(member + step, members), at]
        sums[at] = total

    each(0, groups, add_members)

    def group_copy(step):
        peer = lax.rem(group + step, groups)
        return remote(sums.at[peer], terms.at[group], s2.at[step], r2.at[group], (peer, member))

    def group_wait(step):
        source = lax.rem(group + groups - step, groups)
        remote(
            terms.at[source], terms.at[source], s2.at[step], r2.at[source], (source, member)
        ).wait_recv()

    each(1, groups, lambda step: group_copy(step).start())
    multiply_step(1)
    multiply_across(0)
    travel(2)
    each(1, groups, group_wait)
    total = sums[group]
    for step in range(1, groups):
        total = total + terms[lax.rem(group + step, groups)]
    blocks[own, :rows] = total
    line = lax.broadcasted_iota(jnp.int32, meta.shape, 0)
    blocks[own, rows:] = jnp.where(line == 3, loss, meta[...])
    start, end = spread(groups, members, blocks, *sems)
    start()
    multiply_step(2)
    multiply_across(1)
    for step in range(3, depth):
        travel(step)
        multiply_step(step)
    end()
    for step in range(2, depth):
        multiply_across(step)

    each(1, members, lambda step: member_copy(step).wait_send())
    each(1, groups, lambda step: group_copy(step).wait_send())

    def weights_sent(at):
        slot = at * SIDES + side
        across(slot).wait_send()

        @pl.when((at <= level) & (level < depth - 1))
        def _():
            up(slot).wait_send()

        @pl.when((at >= level) & (level > 0))
        def _():
            down(slot).wait_send()

    each(0, depth, weights_sent)


def project(
    states,
    gain,
    q_weight,
    key_matrix,
    value_matrix,
    queries,
    table,
    positives,
    label_ids,
    kept,
    meta,
    groups,
    members,
):
    tokens, width = states.shape
    batch = queries.shape[0]
    rows, block = batch // members, width // groups
    columns = q_weight.shape[1] + key_matrix.shape[1] + value_matrix.shape[1]
    group_sems = [pltpu.SemaphoreType.DMA((groups,))]
    return pl.pallas_call(
        functools.partial(project_kernel, groups, members),
        out_shape=(
            jax.ShapeDtypeStruct((tokens, columns), jnp.float32),
            jax.ShapeDtypeStruct((batch, table.shape[0]), jnp.bfloat16),
            jax.ShapeDtypeStruct(
                (groups * members, rows + meta.shape[0], block), jnp.float32
            ),
        ),
        in_specs=[pl.BlockSpec(memory_space=pltpu.VMEM)] * 11,
        out_specs=tuple([pl.BlockSpec(memory_space=pltpu.VMEM)] * 3),
        scratch_shapes=[
            pltpu.VMEM((groups, block, columns), jnp.bfloat16),
            pltpu.VMEM((groups, tokens, block), jnp.bfloat16),
            pltpu.VMEM((groups, batch, block), jnp.float32),
            pltpu.VMEM((members, groups, rows, block), jnp.float32),
            pltpu.VMEM((groups, rows, block), jnp.float32),
            pltpu.VMEM((groups, rows, block), jnp.float32),
            *(group_sems * 4),
            pltpu.SemaphoreType.DMA((members,)),
            pltpu.SemaphoreType.DMA((members,)),
            *(group_sems * 2),
            *spread_sems(groups, members),
        ],
        compiler_params=pltpu.CompilerParams(
            collective_id=0, has_side_effects=True, vmem_limit_bytes=48 << 20
        ),
        name="project",
    )(
        states,
        gain,
        q_weight,
        key_matrix,
        value_matrix,
        queries,
        table,
        positives,
        label_ids,
        kept,
        meta,
    )


def tail_kernel(
    groups, members, pooled, weight, base, blocks, pool, terms, parts, s1, r1, s2, r2, *sems
):
    group, member = lax.axis_index("dp"), lax.axis_index("mp")
    own = group * members + member
    devices = groups * members
    share = terms.shape[1]
    barrier = pltpu.get_barrier_semaphore()

    def greet(step):
        peer = lax.rem(own + step, devices)
        pl.semaphore_signal(
            barrier,
            inc=1,
            device_id=(peer // members, lax.rem(peer, members)),
            device_id_type=MESH,
        )

    each(1, devices, greet)
    pl.semaphore_wait(barrier, devices - 1)

    def pool_copy(step):
        peer = lax.rem(group + step, groups)
        return remote(pooled, pool.at[group], s1.at[step], r1.at[group], (peer, member))

    def part_copy(owner_group, owner_member):
        slot = owner_group * members + owner_member
        return remote(
            terms.at[slot], parts.at[own], s2.at[slot], r2.at[own], (owner_group, owner_member)
        )

    def product(at, rows):
        made = jnp.dot(rows, weight[...], preferred_element_type=jnp.float32)
        for index in range(members):
            terms[at * members + index] = made[index * share : (index + 1) * share]

    def project(step):
        at = lax.rem(group + groups - step, groups)
        remote(pooled, pool.at[at], s1.at[step], r1.at[at], (at, member)).wait_recv()
        product(at, pool[at])
        each(0, members, lambda index: part_copy(at, index).start())

    each(1, groups, lambda step: pool_copy(step).start())
    product(group, pooled[...])
    each(1, members, lambda step: part_copy(group, lax.rem(member + step, members)).start())
    parts[own] = terms[own]
    each(1, groups, project)

    def part_wait(step):
        source = lax.rem(own + devices - step, devices)
        remote(
            terms.at[source],
            parts.at[source],
            s2.at[source],
            r2.at[source],
            (source // members, lax.rem(source, members)),
        ).wait_recv()

    each(1, devices, part_wait)
    rows = []
    for at in range(groups):
        total = base[at]
        for index in range(members):
            total = total + parts[at * members + index]
        rows.append(total)
    blocks[own] = jnp.concatenate(rows, axis=0).astype(jnp.bfloat16)
    start, end = spread(groups, members, blocks, *sems)
    start()
    end()
    each(1, groups, lambda step: pool_copy(step).wait_send())

    def part_sent(step):
        slot = lax.rem(own + step, devices)
        part_copy(slot // members, lax.rem(slot, members)).wait_send()

    each(1, devices, part_sent)


def tail(pooled, weight, base, groups, members):
    texts, heads = pooled.shape
    block = weight.shape[1]
    share = texts // members
    devices = groups * members
    return pl.pallas_call(
        functools.partial(tail_kernel, groups, members),
        out_shape=jax.ShapeDtypeStruct((devices, groups * share, block), jnp.bfloat16),
        in_specs=[pl.BlockSpec(memory_space=pltpu.VMEM)] * 3,
        out_specs=pl.BlockSpec(memory_space=pltpu.VMEM),
        scratch_shapes=[
            pltpu.VMEM((groups, texts, heads), jnp.bfloat16),
            pltpu.VMEM((devices, share, block), jnp.float32),
            pltpu.VMEM((devices, share, block), jnp.float32),
            pltpu.SemaphoreType.DMA((groups,)),
            pltpu.SemaphoreType.DMA((groups,)),
            pltpu.SemaphoreType.DMA((devices,)),
            pltpu.SemaphoreType.DMA((devices,)),
            *spread_sems(groups, members),
        ],
        compiler_params=pltpu.CompilerParams(
            collective_id=1, has_side_effects=True, vmem_limit_bytes=24 << 20
        ),
        name="tail",
    )(pooled, weight, base)


def kernels_fit(groups, members, width, share):
    lanes = -(-(width // groups) // 128) * 128
    return members == 4 and groups % SIDES == 0 and groups * members * groups * share * lanes * 2 < 8 << 20


def shards(
    hidden_states,
    token_ids,
    norm_gain,
    q_weight,
    key_matrix,
    value_matrix,
    out_weight,
    label_table,
    refresh_rows,
    label_counts,
    queries,
    positives,
):
    width = hidden_states.shape[1]
    group_tokens = hidden_states.shape[0]
    texts, length = token_ids.shape
    groups = lax.axis_size("dp")
    members = lax.axis_size("mp")
    share = texts // members
    member = lax.axis_index("mp")
    heads = q_weight.shape[1]
    kv = key_matrix.shape[1]
    block = width // groups
    use_kernels = kernels_fit(groups, members, width, share)
    root = math.sqrt(width)
    owned = label_table.shape[0]
    first_label = (lax.axis_index("dp") * members + member) * owned
    label_ids = first_label + jnp.arange(owned, dtype=jnp.int32)
    balance = balances(label_counts)
    replaced = jnp.any(
        refresh_rows[:, None] == jnp.arange(owned, dtype=jnp.int32)[None, :], axis=0
    )
    kept = jnp.where(replaced, 0.0, balance)
    new_ids = first_label + refresh_rows
    new_balance = balances(label_counts[refresh_rows])
    if use_kernels:
        sums = jnp.broadcast_to(jnp.sum(balance), (share,))
        meta = jnp.pad(
            jnp.stack([new_ids.astype(jnp.float32), new_balance, sums]),
            ((0, 5), (0, block - share)),
        )
        raw, early_slopes, reduced = project(
            hidden_states,
            norm_gain[None, :],
            q_weight,
            key_matrix,
            value_matrix,
            queries,
            label_table,
            positives,
            label_ids[None, :],
            kept[None, :],
            meta,
            groups,
            members,
        )
        rows = queries.shape[0] // members
        query_sum = (
            reduced[:, :rows]
            .reshape(groups, members, rows, block)
            .transpose(1, 2, 0, 3)
            .reshape(queries.shape[0], width)
        )
        new_ids = reduced[:, rows, :share].reshape(-1).astype(jnp.int32)
        new_balance = reduced[:, rows + 1, :share].reshape(-1)
        summed_weight = jnp.sum(reduced[:, rows + 2, 0])
        loss_sum = jnp.sum(reduced[:, rows + 3, 0])
    else:
        states = hidden_states.astype(jnp.float32)
        scaled = lax.rsqrt(jnp.mean(states * states, axis=1, keepdims=True) + norm_eps)
        normed = (states * scaled * norm_gain).astype(jnp.bfloat16)
        weights = lax.all_gather(
            jnp.concatenate([q_weight, key_matrix, value_matrix], axis=1),
            "dp",
            axis=0,
            tiled=True,
        )
        raw = jnp.dot(normed, weights, preferred_element_type=jnp.float32)
        early_slopes, early_loss = focal(queries, label_table, positives, label_ids, kept, root)
        query_part = jnp.dot(early_slopes, label_table, preferred_element_type=jnp.float32) / root
        query_sum, loss_sum, summed_weight = lax.psum(
            (query_part, early_loss, jnp.sum(balance)), ("dp", "mp")
        )
        new_ids = lax.all_gather(new_ids, ("dp", "mp"), axis=0, tiled=True)
        new_balance = lax.all_gather(new_balance, ("dp", "mp"), axis=0, tiled=True)
    query_raw = raw[:, :heads]
    key_raw = raw[:, heads : heads + kv]
    value_raw = raw[:, heads + kv :]
    queries_rot = (
        rotary(query_raw.reshape(texts, length, -1, HEAD_WIDTH), HEAD_WIDTH)
        .reshape(group_tokens, -1)
        .astype(jnp.bfloat16)
    )
    rotary_keys = (
        rotary(key_raw.reshape(texts, length, -1, HEAD_WIDTH), HEAD_WIDTH)
        .reshape(group_tokens, -1)
        .astype(jnp.bfloat16)
    )
    values_rot = value_raw.astype(jnp.bfloat16)
    attended = attend(queries_rot, rotary_keys, values_rot, token_ids, HEAD_WIDTH)
    live = (token_ids != 0).astype(jnp.float32)
    counted = jnp.sum(live, axis=1, keepdims=True)
    pooled = (
        jnp.sum(attended.astype(jnp.float32).reshape(texts, length, -1) * live[:, :, None], axis=1)
        / counted
    ).astype(jnp.bfloat16)
    live_own = lax.dynamic_slice_in_dim(live, member * share, share, 0)
    states_own = lax.dynamic_slice_in_dim(
        hidden_states, member * share * length, share * length, 0
    ).reshape(share, length, width)
    counted_own = jnp.sum(live_own, axis=1, keepdims=True)
    base_own = (
        jnp.sum(states_own.astype(jnp.float32) * live_own[:, :, None], axis=1) / counted_own
    )
    if use_kernels:
        base_blocks = jnp.swapaxes(base_own.reshape(share, groups, block), 0, 1)
        gathered = tail(pooled, out_weight.T, base_blocks, groups, members)
        refreshed_all = jnp.swapaxes(
            gathered.reshape(groups * members, groups, share, block), 1, 2
        ).reshape(groups * members * share, width)
    else:
        refreshed_all = gather_refreshed(pooled, out_weight, base_own, groups, members)

    late_slopes, late_loss = focal(queries, refreshed_all, positives, new_ids, new_balance, root)
    query_late = jnp.dot(late_slopes, refreshed_all, preferred_element_type=jnp.float32) / root
    own_late = lax.dynamic_slice_in_dim(
        late_slopes, (lax.axis_index("dp") * members + member) * share, share, 1
    )
    slopes = early_slopes.at[:, refresh_rows].set(own_late)
    label_part = (
        lax.dot_general(
            slopes, queries, (((0,), (0,)), ((), ())), preferred_element_type=jnp.float32
        )
        / root
    )
    total_labels = owned * groups * members
    factor = total_labels / summed_weight
    loss = factor * (loss_sum + late_loss) / (queries.shape[0] * total_labels)
    return (factor * label_part, factor * (query_sum + query_late), loss)


def gather_refreshed(pooled, out_weight, base_own, groups, members):
    share, width = base_own.shape
    pooled_all = lax.all_gather(pooled, "dp", axis=0, tiled=True)
    terms = lax.dot_general(
        pooled_all, out_weight, (((1,), (1,)), ((), ())), preferred_element_type=jnp.float32
    ).reshape(groups, members, share, -1)
    mine = lax.psum_scatter(terms, "mp", scatter_dimension=1, tiled=True)
    swapped = lax.all_to_all(mine.reshape(groups, share, -1), "dp", 0, 0, tiled=True)
    projected = jnp.swapaxes(swapped, 0, 1).reshape(share, width)
    refreshed = (base_own + projected).astype(jnp.bfloat16)
    return lax.all_gather(refreshed, ("dp", "mp"), axis=0, tiled=True)


def balances(label_counts):
    return (1.0 - focal_beta) / -jnp.expm1(
        label_counts.astype(jnp.float32) * math.log(focal_beta)
    )


def focal(queries, table, positives, label_ids, balance, root):
    logits = (
        lax.dot_general(
            queries, table, (((1,), (1,)), ((), ())), preferred_element_type=jnp.float32
        )
        / root
    )
    matched = jnp.any(positives[:, :, None] == label_ids[None, None, :], axis=1)
    signs = jnp.where(matched, 1.0, -1.0)
    margin = signs * logits
    missed = jax.nn.sigmoid(-margin)
    softened = jax.nn.softplus(-margin)
    loss = jnp.sum(balance[None, :] * missed * missed * softened)
    slopes = (
        balance[None, :]
        * signs
        * (-(missed * missed) * (2.0 * jax.nn.sigmoid(margin) * softened + missed))
    ).astype(jnp.bfloat16)
    return slopes, loss


def solution(mesh):
    in_specs = (
        P("dp", None),
        P("dp", None),
        P(),
        P("dp", "mp"),
        P("dp", "mp"),
        P("dp", "mp"),
        P("dp", "mp"),
        P(("dp", "mp"), None),
        P(("dp", "mp")),
        P(("dp", "mp")),
        P(),
        P(),
    )
    out_specs = (P(("dp", "mp"), None), P(), P())
    return jax.shard_map(shards, mesh=mesh, in_specs=in_specs, out_specs=out_specs, check_vma=False)
```

```python
import functools
import math

import jax
import jax.numpy as jnp
from jax import lax
from jax.experimental import pallas as pl
from jax.experimental.pallas import tpu as pltpu
from jax.sharding import PartitionSpec as P

MESH = pl.DeviceIdType.MESH
SIDES = 2

HEAD_WIDTH = 128


rope_theta = 1000000.0
norm_eps = 1e-06
focal_beta = 0.9999


def rotary(values, head_size):
    length = values.shape[1]
    half = head_size // 2
    frequency = rope_theta ** (-2.0 * jnp.arange(half, dtype=jnp.float32) / head_size)
    angles = jnp.arange(length, dtype=jnp.float32)[:, None] * frequency[None, :]
    cosine = jnp.concatenate([jnp.cos(angles), jnp.cos(angles)], axis=1)[None, :, None, :]
    sine = jnp.concatenate([jnp.sin(angles), jnp.sin(angles)], axis=1)[None, :, None, :]
    turned = jnp.concatenate([-values[..., half:], values[..., :half]], axis=-1)
    return values * cosine + turned * sine


def attend(query_rows, key_rows, value_rows, text_ids, head_size):
    texts, length = text_ids.shape
    kv_heads = key_rows.shape[1] // head_size
    repeat = query_rows.shape[1] // head_size // kv_heads
    query_r = query_rows.reshape(texts, length, kv_heads, repeat, head_size)
    key_r = key_rows.reshape(texts, length, kv_heads, head_size)
    value_r = value_rows.reshape(texts, length, kv_heads, head_size)
    scores = jnp.einsum(
        "ntgrd,nsgd->ngrts", query_r, key_r, preferred_element_type=jnp.float32
    ) / math.sqrt(head_size)
    causal = jnp.arange(length)[:, None] >= jnp.arange(length)[None, :]
    allowed = causal[None, None, None, :, :] & (text_ids != 0)[:, None, None, None, :]
    weights = jnp.where(allowed, jnp.exp(scores), 0.0)
    probs = (weights / jnp.sum(weights, axis=-1, keepdims=True)).astype(jnp.bfloat16)
    mixed = jnp.einsum("ngrts,nsgd->ntgrd", probs, value_r, preferred_element_type=jnp.float32)
    return mixed.reshape(texts * length, -1).astype(jnp.bfloat16)


def remote(source, target, send, receive, device):
    return pltpu.make_async_remote_copy(
        src_ref=source,
        dst_ref=target,
        send_sem=send,
        recv_sem=receive,
        device_id=device,
        device_id_type=MESH,
    )


def each(low, high, body):
    def run(index, carry):
        body(index)
        return carry

    lax.fori_loop(low, high, run, 0)


def slopes_of(logits, positives, label_ids, balance):
    matched = positives[:, 0:1] == label_ids
    for index in range(1, positives.shape[1]):
        matched = matched | (positives[:, index : index + 1] == label_ids)
    signs = jnp.where(matched, 1.0, -1.0)
    margin = signs * logits
    small = jnp.exp(-jnp.abs(margin))
    larger, smaller = 1.0 / (1.0 + small), small / (1.0 + small)
    missed = jnp.where(margin >= 0.0, smaller, larger)
    hit = jnp.where(margin >= 0.0, larger, smaller)
    softened = jnp.maximum(-margin, 0.0) + jnp.log1p(small)
    loss = jnp.sum(balance * missed * missed * softened)
    made = balance * signs * (-(missed * missed) * (2.0 * hit * softened + missed))
    return made.astype(jnp.bfloat16), loss


def spread(groups, members, blocks, group_sem, far_sem, core_sem, relay_sem, arrived):
    group, member = lax.axis_index("dp"), lax.axis_index("mp")
    far = lax.rem(member + 2, members)
    core = member + 1 - 2 * lax.rem(member, 2)
    far_core = lax.rem(core + 2, members)

    def copy(at, slot, sems, index, device):
        return remote(blocks.at[slot], blocks.at[slot], sems.at[index], arrived.at[slot], device)

    def forward(at):
        slot = at * members + member
        copy(at, slot, far_sem, at, (group, far)).start()
        copy(at, slot, core_sem, at, (group, core)).start()

    def send(step):
        slot = group * members + member
        copy(group, slot, group_sem, step, (lax.rem(group + step, groups), member)).start()

    def pass_on(step):
        at = lax.rem(group + groups - step, groups)
        slot = at * members + member
        copy(at, slot, group_sem, step, (at, member)).wait_recv()
        forward(at)

    def relay(step):
        at = lax.rem(group + groups - step, groups)
        slot = at * members + far
        copy(at, slot, far_sem, at, (group, far)).wait_recv()
        copy(at, slot, relay_sem, at, (group, core)).start()

    def finish(at):
        copy(at, at * members + core, core_sem, at, (group, core)).wait_recv()
        copy(at, at * members + far_core, relay_sem, at, (group, core)).wait_recv()
        copy(at, at * members + member, far_sem, at, (group, far)).wait_send()
        copy(at, at * members + member, core_sem, at, (group, core)).wait_send()
        copy(at, at * members + far, relay_sem, at, (group, core)).wait_send()

    def sent(step):
        slot = group * members + member
        copy(group, slot, group_sem, step, (lax.rem(group + step, groups), member)).wait_send()

    def start():
        each(1, groups, send)
        forward(group)

    def end():
        each(1, groups, pass_on)
        each(0, groups, relay)
        each(0, groups, finish)
        each(1, groups, sent)

    return start, end


def spread_sems(groups, members):
    return [
        pltpu.SemaphoreType.DMA((groups,)),
        pltpu.SemaphoreType.DMA((groups,)),
        pltpu.SemaphoreType.DMA((groups,)),
        pltpu.SemaphoreType.DMA((groups,)),
        pltpu.SemaphoreType.DMA((groups * members,)),
    ]


def project_kernel(
    groups,
    members,
    states_far,
    q_weight,
    key_matrix,
    value_matrix,
    queries_far,
    table_far,
    gain,
    positives,
    label_ids,
    kept,
    meta,
    ids,
    turns,
    pooled,
    base,
    slopes,
    blocks,
    states,
    queries,
    table,
    raw,
    pools,
    weights,
    normed,
    part,
    got,
    sums,
    terms,
    local_sem,
    up_sem,
    down_sem,
    side_sem,
    landed,
    s1,
    r1,
    s2,
    r2,
    *sems,
):
    group, member = lax.axis_index("dp"), lax.axis_index("mp")
    own = group * members + member
    depth = groups // SIDES
    level, side = group // SIDES, lax.rem(group, SIDES)
    block = table.shape[1] // groups
    rows = queries.shape[0] // members
    heads, kv = q_weight.shape[1], key_matrix.shape[1]
    barrier = pltpu.get_barrier_semaphore()

    def greet_member(step):
        peer = lax.rem(member + step, members)
        pl.semaphore_signal(barrier, inc=1, device_id=(group, peer), device_id_type=MESH)

    def greet_group(step):
        peer = lax.rem(group + step, groups)
        pl.semaphore_signal(barrier, inc=1, device_id=(peer, member), device_id_type=MESH)

    held = weights.at[group]
    fetches = [
        pltpu.make_async_copy(source, target, local_sem.at[index])
        for index, (source, target) in enumerate(
            (
                (q_weight, held.at[:, pl.ds(0, heads)]),
                (key_matrix, held.at[:, pl.ds(heads, kv)]),
                (value_matrix, held.at[:, pl.ds(heads + kv, kv)]),
                (queries_far, queries),
                (table_far, table),
                (states_far, states),
            )
        )
    ]
    for fetch in fetches:
        fetch.start()
    each(1, members, greet_member)
    each(1, groups, greet_group)
    for fetch in fetches[:3]:
        fetch.wait()
    pl.semaphore_wait(barrier, groups + members - 2)

    def weight_copy(slot, sem, peer):
        return remote(
            weights.at[slot], weights.at[slot], sem.at[slot], landed.at[slot], (peer, member)
        )

    def up(slot):
        return weight_copy(slot, up_sem, group + SIDES)

    def down(slot):
        return weight_copy(slot, down_sem, group - SIDES)

    def across(slot):
        return weight_copy(slot, side_sem, level * SIDES + 1 - side)

    def travel(step):
        @pl.when(level >= step)
        def _():
            slot = group - step * SIDES
            if step > 0:
                weight_copy(slot, down_sem, group - SIDES).wait_recv()

            @pl.when(level < depth - 1)
            def _():
                up(slot).start()

            across(slot).start()

        if step == 0:

            @pl.when(level > 0)
            def _():
                down(group).start()

        else:

            @pl.when(level + step < depth)
            def _():
                slot = group + step * SIDES
                weight_copy(slot, up_sem, group + SIDES).wait_recv()

                @pl.when(level > 0)
                def _():
                    down(slot).start()

                across(slot).start()

    tokens = states.shape[0]
    tile = 128 if tokens % 128 == 0 else tokens

    def multiply(slot):
        def some(index):
            at = pl.ds(pl.multiple_of(index * tile, tile), tile)
            raw[at, :] += jnp.dot(
                normed[slot, at, :], weights[slot], preferred_element_type=jnp.float32
            )

        each(0, tokens // tile, some)

    def multiply_step(step):
        @pl.when(level >= step)
        def _():
            multiply(group - step * SIDES)

        if step > 0:

            @pl.when(level + step < depth)
            def _():
                multiply(group + step * SIDES)

    def multiply_across(step):
        def one(at):
            slot = at * SIDES + 1 - side
            across(slot).wait_recv()
            multiply(slot)

        @pl.when(level >= step)
        def _():
            one(level - step)

        if step > 0:

            @pl.when(level + step < depth)
            def _():
                one(level + step)

    travel(0)
    for fetch in fetches[3:]:
        fetch.wait()

    root = math.sqrt(table.shape[1])
    logits = (
        lax.dot_general(
            queries[...],
            table[...],
            (((1,), (1,)), ((), ())),
            preferred_element_type=jnp.float32,
        )
        / root
    )
    early, loss = slopes_of(logits, positives[...], label_ids[...], kept[...])
    slopes[...] = early
    for at in range(groups):
        part[at] = (
            jnp.dot(
                early,
                table[:, at * block : (at + 1) * block],
                preferred_element_type=jnp.float32,
            )
            / root
        )

    def member_copy(step):
        peer = lax.rem(member + step, members)
        start = pl.multiple_of(peer * rows, rows)
        return remote(
            part.at[:, pl.ds(start, rows), :],
            got.at[member],
            s1.at[step],
            r1.at[member],
            (group, peer),
        )

    def member_wait(step):
        source = lax.rem(member + members - step, members)
        remote(
            got.at[source], got.at[source], s1.at[step], r1.at[source], (group, source)
        ).wait_recv()

    each(1, members, lambda step: member_copy(step).start())

    def normalize(index):
        at = pl.ds(pl.multiple_of(index * 64, 64), 64)
        wide = states[at, :].astype(jnp.float32)
        scaled = lax.rsqrt(jnp.mean(wide * wide, axis=1, keepdims=True) + norm_eps)
        ready = (wide * scaled * gain[...]).astype(jnp.bfloat16)
        for piece in range(groups):
            normed[piece, at, :] = ready[:, piece * block : (piece + 1) * block]

    each(0, tokens // 64, normalize)
    texts, length = pooled.shape[0], tokens // pooled.shape[0]
    chunk, share = tokens // members, texts // members

    def living(index):
        live = ids[index] != 0
        row = lax.broadcasted_iota(jnp.int32, (share, chunk), 0)
        column = lax.broadcasted_iota(jnp.int32, (share, chunk), 1)
        chosen = jnp.where((lax.div(column, length) == row) & live, 1.0, 0.0)
        return chosen.astype(jnp.bfloat16), jnp.sum(chosen, axis=1, keepdims=True)

    chosen, counted = living(member)
    mine = pl.ds(pl.multiple_of(member * chunk, chunk), chunk)
    for at in range(groups):
        base[at] = (
            jnp.dot(
                chosen,
                states[mine, at * block : (at + 1) * block],
                preferred_element_type=jnp.float32,
            )
            / counted
        )
    raw[...] = jnp.zeros_like(raw)
    multiply_step(0)
    travel(1)
    each(1, members, member_wait)
    first = pl.multiple_of(member * rows, rows)

    def add_members(at):
        total = part[at, pl.ds(first, rows), :]
        for step in range(1, members):
            total = total + got[lax.rem(member + step, members), at]
        sums[at] = total

    each(0, groups, add_members)

    def group_copy(step):
        peer = lax.rem(group + step, groups)
        return remote(sums.at[peer], terms.at[group], s2.at[step], r2.at[group], (peer, member))

    def group_wait(step):
        source = lax.rem(group + groups - step, groups)
        remote(
            terms.at[source], terms.at[source], s2.at[step], r2.at[source], (source, member)
        ).wait_recv()

    each(1, groups, lambda step: group_copy(step).start())
    multiply_step(1)
    multiply_across(0)
    travel(2)
    each(1, groups, group_wait)
    total = sums[group]
    for step in range(1, groups):
        total = total + terms[lax.rem(group + step, groups)]
    blocks[own, :rows] = total
    line = lax.broadcasted_iota(jnp.int32, meta.shape, 0)
    blocks[own, rows:] = jnp.where(line == 3, loss, meta[...])
    start, end = spread(groups, members, blocks, *sems)
    start()
    multiply_step(2)
    multiply_across(1)
    for step in range(3, depth):
        travel(step)
        multiply_step(step)
    end()
    for step in range(2, depth):
        multiply_across(step)

    def attend_some(index):
        at = pl.ds(pl.multiple_of(index * chunk, chunk), chunk)

        def rotate(values):
            turned = pltpu.roll(values, HEAD_WIDTH // 2, 1)
            return (values * turns[0] + turned * turns[1]).astype(jnp.bfloat16)

        row = lax.broadcasted_iota(jnp.int32, (chunk, chunk), 0)
        column = lax.broadcasted_iota(jnp.int32, (chunk, chunk), 1)
        allowed = (lax.div(row, length) == lax.div(column, length)) & (column <= row)
        allowed = allowed & (ids[index] != 0)
        chosen, counted = living(index)
        repeat = heads // kv
        out = pl.ds(pl.multiple_of(index * share, share), share)
        for head in range(heads // HEAD_WIDTH):
            if head % repeat == 0:
                start = heads + head // repeat * HEAD_WIDTH
                keys = rotate(raw[at, start : start + HEAD_WIDTH])
                values = raw[at, start + kv : start + kv + HEAD_WIDTH].astype(jnp.bfloat16)
            columns = slice(head * HEAD_WIDTH, (head + 1) * HEAD_WIDTH)
            scores = lax.dot_general(
                rotate(raw[at, columns]),
                keys,
                (((1,), (1,)), ((), ())),
                preferred_element_type=jnp.float32,
            ) / math.sqrt(HEAD_WIDTH)
            made = jnp.where(allowed, jnp.exp(scores), 0.0)
            probs = (made / jnp.sum(made, axis=1, keepdims=True)).astype(jnp.bfloat16)
            mixed = jnp.dot(probs, values, preferred_element_type=jnp.float32)
            pools[out, columns] = (
                jnp.dot(chosen, mixed.astype(jnp.bfloat16), preferred_element_type=jnp.float32)
                / counted
            )

    each(0, members, attend_some)
    pooled[...] = pools[...].astype(jnp.bfloat16)

    each(1, members, lambda step: member_copy(step).wait_send())
    each(1, groups, lambda step: group_copy(step).wait_send())

    def weights_sent(at):
        slot = at * SIDES + side
        across(slot).wait_send()

        @pl.when((at <= level) & (level < depth - 1))
        def _():
            up(slot).wait_send()

        @pl.when((at >= level) & (level > 0))
        def _():
            down(slot).wait_send()

    each(0, depth, weights_sent)


def project(
    states,
    q_weight,
    key_matrix,
    value_matrix,
    queries,
    table,
    gain,
    positives,
    label_ids,
    kept,
    meta,
    ids,
    turns,
    groups,
    members,
):
    tokens, width = states.shape
    batch = queries.shape[0]
    heads = q_weight.shape[1]
    texts = members * (meta.shape[0])
    rows, block = batch // members, width // groups
    columns = heads + key_matrix.shape[1] + value_matrix.shape[1]
    group_sems = [pltpu.SemaphoreType.DMA((groups,))]
    return pl.pallas_call(
        functools.partial(project_kernel, groups, members),
        out_shape=(
            jax.ShapeDtypeStruct((texts, heads), jnp.bfloat16),
            jax.ShapeDtypeStruct((groups, texts // members, block), jnp.float32),
            jax.ShapeDtypeStruct((batch, table.shape[0]), jnp.bfloat16),
            jax.ShapeDtypeStruct(
                (groups * members, rows + meta.shape[0], block), jnp.float32
            ),
        ),
        in_specs=[pl.BlockSpec(memory_space=pl.ANY)] * 6
        + [pl.BlockSpec(memory_space=pltpu.VMEM)] * 7,
        out_specs=tuple([pl.BlockSpec(memory_space=pltpu.VMEM)] * 4),
        scratch_shapes=[
            pltpu.VMEM(states.shape, jnp.bfloat16),
            pltpu.VMEM(queries.shape, jnp.bfloat16),
            pltpu.VMEM(table.shape, jnp.bfloat16),
            pltpu.VMEM((tokens, columns), jnp.float32),
            pltpu.VMEM((texts, heads), jnp.float32),
            pltpu.VMEM((groups, block, columns), jnp.bfloat16),
            pltpu.VMEM((groups, tokens, block), jnp.bfloat16),
            pltpu.VMEM((groups, batch, block), jnp.float32),
            pltpu.VMEM((members, groups, rows, block), jnp.float32),
            pltpu.VMEM((groups, rows, block), jnp.float32),
            pltpu.VMEM((groups, rows, block), jnp.float32),
            pltpu.SemaphoreType.DMA((6,)),
            *(group_sems * 4),
            pltpu.SemaphoreType.DMA((members,)),
            pltpu.SemaphoreType.DMA((members,)),
            *(group_sems * 2),
            *spread_sems(groups, members),
        ],
        compiler_params=pltpu.CompilerParams(
            collective_id=0, has_side_effects=True, vmem_limit_bytes=48 << 20
        ),
        name="project",
    )(
        states,
        q_weight,
        key_matrix,
        value_matrix,
        queries,
        table,
        gain,
        positives,
        label_ids,
        kept,
        meta,
        ids,
        turns,
    )


def tail_kernel(
    groups,
    members,
    owned,
    pooled,
    weight,
    base,
    queries,
    positives,
    early,
    reduced,
    query_out,
    slopes,
    scalars,
    blocks,
    pool,
    terms,
    parts,
    rows_wide,
    s1,
    r1,
    s2,
    r2,
    *sems,
):
    group, member = lax.axis_index("dp"), lax.axis_index("mp")
    own = group * members + member
    devices = groups * members
    share = terms.shape[1]
    barrier = pltpu.get_barrier_semaphore()

    def greet(step):
        peer = lax.rem(own + step, devices)
        pl.semaphore_signal(
            barrier,
            inc=1,
            device_id=(peer // members, lax.rem(peer, members)),
            device_id_type=MESH,
        )

    each(1, devices, greet)
    pl.semaphore_wait(barrier, devices - 1)

    def pool_copy(step):
        peer = lax.rem(group + step, groups)
        return remote(pooled, pool.at[group], s1.at[step], r1.at[group], (peer, member))

    def part_copy(owner_group, owner_member):
        slot = owner_group * members + owner_member
        return remote(
            terms.at[slot], parts.at[own], s2.at[slot], r2.at[own], (owner_group, owner_member)
        )

    def product(at, rows):
        made = jnp.dot(rows, weight[...], preferred_element_type=jnp.float32)
        for index in range(members):
            terms[at * members + index] = made[index * share : (index + 1) * share]

    def project(step):
        at = lax.rem(group + groups - step, groups)
        remote(pooled, pool.at[at], s1.at[step], r1.at[at], (at, member)).wait_recv()
        product(at, pool[at])
        each(0, members, lambda index: part_copy(at, index).start())

    each(1, groups, lambda step: pool_copy(step).start())
    product(group, pooled[...])
    each(1, members, lambda step: part_copy(group, lax.rem(member + step, members)).start())
    parts[own] = terms[own]
    each(1, groups, project)

    def part_wait(step):
        source = lax.rem(own + devices - step, devices)
        remote(
            terms.at[source],
            parts.at[source],
            s2.at[source],
            r2.at[source],
            (source // members, lax.rem(source, members)),
        ).wait_recv()

    each(1, devices, part_wait)
    rows = []
    for at in range(groups):
        total = base[at]
        for index in range(members):
            total = total + parts[at * members + index]
        rows.append(total)
    blocks[own] = jnp.concatenate(rows, axis=0).astype(jnp.bfloat16)
    start, end = spread(groups, members, blocks, *sems)
    start()
    texts = devices * share
    block = base.shape[2]
    batch = queries.shape[0]
    height = batch // members
    notes = reduced[0, height:, :]
    for at in range(1, devices):
        notes = notes + reduced[at, height:, :]
    new_ids = notes[0:1, :texts].astype(jnp.int32)
    scalars[...] = notes[:, :128]
    end()

    def widen(at):
        wide = blocks[at].astype(jnp.float32)
        for piece in range(groups):
            rows_wide[piece, pl.ds(pl.multiple_of(at * share, share), share), :] = wide[
                piece * share : (piece + 1) * share
            ]

    each(0, devices, widen)
    root = math.sqrt(groups * block)
    logits = jnp.zeros((batch, texts), jnp.float32)
    for piece in range(groups):
        logits = logits + lax.dot_general(
            queries[:, piece * block : (piece + 1) * block],
            rows_wide[piece].astype(jnp.bfloat16),
            (((1,), (1,)), ((), ())),
            preferred_element_type=jnp.float32,
        )
    late, loss = slopes_of(logits / root, positives[...], new_ids, notes[1:2, :texts])
    line = lax.broadcasted_iota(jnp.int32, scalars.shape, 0)
    scalars[...] = scalars[...] + jnp.where(line == 3, loss, 0.0)
    for piece in range(groups):
        made = (
            jnp.dot(
                late, rows_wide[piece].astype(jnp.bfloat16), preferred_element_type=jnp.float32
            )
            / root
        )
        for index in range(members):
            query_out[
                index * height : (index + 1) * height, piece * block : (piece + 1) * block
            ] = (
                made[index * height : (index + 1) * height]
                + reduced[piece * members + index, :height, :]
            )
    labels = own * owned + lax.broadcasted_iota(jnp.int32, (owned, texts), 0)
    place = jnp.where(labels == new_ids, 1.0, 0.0).astype(jnp.bfloat16)
    moved = lax.dot_general(
        late, place, (((1,), (1,)), ((), ())), preferred_element_type=jnp.float32
    )
    slopes[...] = (early[...].astype(jnp.float32) + moved).astype(jnp.bfloat16)
    each(1, groups, lambda step: pool_copy(step).wait_send())

    def part_sent(step):
        slot = lax.rem(own + step, devices)
        part_copy(slot // members, lax.rem(slot, members)).wait_send()

    each(1, devices, part_sent)


def tail(pooled, weight, base, queries, positives, early, reduced, groups, members):
    texts, heads = pooled.shape
    block = weight.shape[1]
    share = texts // members
    devices = groups * members
    return pl.pallas_call(
        functools.partial(tail_kernel, groups, members, early.shape[1]),
        out_shape=(
            jax.ShapeDtypeStruct(queries.shape, jnp.float32),
            jax.ShapeDtypeStruct(early.shape, jnp.bfloat16),
            jax.ShapeDtypeStruct((8, 128), jnp.float32),
        ),
        in_specs=[pl.BlockSpec(memory_space=pltpu.VMEM)] * 7,
        out_specs=tuple([pl.BlockSpec(memory_space=pltpu.VMEM)] * 3),
        scratch_shapes=[
            pltpu.VMEM((devices, groups * share, block), jnp.bfloat16),
            pltpu.VMEM((groups, texts, heads), jnp.bfloat16),
            pltpu.VMEM((devices, share, block), jnp.float32),
            pltpu.VMEM((devices, share, block), jnp.float32),
            pltpu.VMEM((groups, devices * share, block), jnp.float32),
            pltpu.SemaphoreType.DMA((groups,)),
            pltpu.SemaphoreType.DMA((groups,)),
            pltpu.SemaphoreType.DMA((devices,)),
            pltpu.SemaphoreType.DMA((devices,)),
            *spread_sems(groups, members),
        ],
        compiler_params=pltpu.CompilerParams(
            collective_id=1, has_side_effects=True, vmem_limit_bytes=40 << 20
        ),
        name="tail",
    )(pooled, weight, base, queries, positives, early, reduced)


def kernels_fit(groups, members, width, share):
    lanes = -(-(width // groups) // 128) * 128
    return (
        members == 4
        and share == 8
        and groups % SIDES == 0
        and groups * members * share <= width // groups
        and groups * members * groups * share * lanes * 2 < 8 << 20
    )


def shards(
    hidden_states,
    token_ids,
    norm_gain,
    q_weight,
    key_matrix,
    value_matrix,
    out_weight,
    label_table,
    refresh_rows,
    label_counts,
    queries,
    positives,
):
    width = hidden_states.shape[1]
    texts, length = token_ids.shape
    groups = lax.axis_size("dp")
    members = lax.axis_size("mp")
    share = texts // members
    if not kernels_fit(groups, members, width, share):
        return plain_shards(
            hidden_states,
            token_ids,
            norm_gain,
            q_weight,
            key_matrix,
            value_matrix,
            out_weight,
            label_table,
            refresh_rows,
            label_counts,
            queries,
            positives,
        )
    block = width // groups
    root = math.sqrt(width)
    owned = label_table.shape[0]
    own = lax.axis_index("dp") * members + lax.axis_index("mp")
    first_label = own * owned
    label_ids = first_label + jnp.arange(owned, dtype=jnp.int32)
    balance = balances(label_counts)
    replaced = refresh_rows[:, None] == jnp.arange(owned, dtype=jnp.int32)[None, :]
    kept = jnp.where(jnp.any(replaced, axis=0), 0.0, balance)
    lanes = jnp.arange(block, dtype=jnp.int32)
    here = (lanes // share) == own
    spot = lanes % share
    picked = (spot[None, :] == jnp.arange(share, dtype=jnp.int32)[:, None]) & here[None, :]
    new_balance = jnp.sum(jnp.where(replaced, balance[None, :], 0.0), axis=1)
    new_ids = (first_label + refresh_rows).astype(jnp.float32)
    meta = jnp.concatenate(
        [
            jnp.sum(jnp.where(picked, new_ids[:, None], 0.0), axis=0, keepdims=True),
            jnp.sum(jnp.where(picked, new_balance[:, None], 0.0), axis=0, keepdims=True),
            jnp.broadcast_to(jnp.sum(balance), (1, block)),
            jnp.zeros((5, block), jnp.float32),
        ],
        axis=0,
    )
    half = HEAD_WIDTH // 2
    frequency = rope_theta ** (-2.0 * jnp.arange(half, dtype=jnp.float32) / HEAD_WIDTH)
    places = jnp.arange(share * length, dtype=jnp.int32) % length
    angles = places.astype(jnp.float32)[:, None] * frequency[None, :]
    cosine, sine = jnp.cos(angles), jnp.sin(angles)
    turns = jnp.stack(
        [
            jnp.concatenate([cosine, cosine], axis=1),
            jnp.concatenate([-sine, sine], axis=1),
        ]
    )
    pooled, base, early, reduced = project(
        hidden_states,
        q_weight,
        key_matrix,
        value_matrix,
        queries,
        label_table,
        norm_gain[None, :],
        positives,
        label_ids[None, :],
        kept[None, :],
        meta,
        token_ids.reshape(members, 1, share * length),
        turns,
        groups,
        members,
    )
    query_sum, slopes, scalars = tail(
        pooled, out_weight.T, base, queries, positives, early, reduced, groups, members
    )
    total_labels = owned * groups * members
    factor = total_labels / scalars[2, 0]
    loss = factor * scalars[3, 0] / (queries.shape[0] * total_labels)
    label_part = (
        lax.dot_general(
            slopes, queries, (((0,), (0,)), ((), ())), preferred_element_type=jnp.float32
        )
        / root
    )
    return (factor * label_part, factor * query_sum, loss)


def plain_shards(
    hidden_states,
    token_ids,
    norm_gain,
    q_weight,
    key_matrix,
    value_matrix,
    out_weight,
    label_table,
    refresh_rows,
    label_counts,
    queries,
    positives,
):
    width = hidden_states.shape[1]
    group_tokens = hidden_states.shape[0]
    texts, length = token_ids.shape
    states = hidden_states.astype(jnp.float32)
    scaled = lax.rsqrt(jnp.mean(states * states, axis=1, keepdims=True) + norm_eps)
    normed = (states * scaled * norm_gain).astype(jnp.bfloat16)
    heads = q_weight.shape[1]
    kv = key_matrix.shape[1]
    weights = lax.all_gather(
        jnp.concatenate([q_weight, key_matrix, value_matrix], axis=1), "dp", axis=0, tiled=True
    )
    raw = jnp.dot(normed, weights, preferred_element_type=jnp.float32)
    query_raw = raw[:, :heads]
    key_raw = raw[:, heads : heads + kv]
    value_raw = raw[:, heads + kv :]
    queries_rot = (
        rotary(query_raw.reshape(texts, length, -1, HEAD_WIDTH), HEAD_WIDTH)
        .reshape(group_tokens, -1)
        .astype(jnp.bfloat16)
    )
    rotary_keys = (
        rotary(key_raw.reshape(texts, length, -1, HEAD_WIDTH), HEAD_WIDTH)
        .reshape(group_tokens, -1)
        .astype(jnp.bfloat16)
    )
    values_rot = value_raw.astype(jnp.bfloat16)
    attended = attend(queries_rot, rotary_keys, values_rot, token_ids, HEAD_WIDTH)
    live = (token_ids != 0).astype(jnp.float32)
    counted = jnp.sum(live, axis=1, keepdims=True)
    pooled = (
        jnp.sum(attended.astype(jnp.float32).reshape(texts, length, -1) * live[:, :, None], axis=1)
        / counted
    ).astype(jnp.bfloat16)
    groups = lax.axis_size("dp")
    members = lax.axis_size("mp")
    share = texts // members
    member = lax.axis_index("mp")
    live_own = lax.dynamic_slice_in_dim(live, member * share, share, 0)
    states_own = lax.dynamic_slice_in_dim(
        hidden_states, member * share * length, share * length, 0
    ).reshape(share, length, width)
    counted_own = jnp.sum(live_own, axis=1, keepdims=True)
    base_own = (
        jnp.sum(states_own.astype(jnp.float32) * live_own[:, :, None], axis=1) / counted_own
    )
    pooled_all = lax.all_gather(pooled, "dp", axis=0, tiled=True)
    terms = lax.dot_general(
        pooled_all, out_weight, (((1,), (1,)), ((), ())), preferred_element_type=jnp.float32
    ).reshape(groups, members, share, -1)
    mine = lax.psum_scatter(terms, "mp", scatter_dimension=1, tiled=True)
    mine = mine.reshape(groups, share, -1)
    swapped = lax.all_to_all(mine, "dp", 0, 0, tiled=True)
    projected = jnp.swapaxes(swapped, 0, 1).reshape(share, width)
    refreshed = (base_own + projected).astype(jnp.bfloat16)

    root = math.sqrt(width)
    owned = label_table.shape[0]
    first_label = (lax.axis_index("dp") * members + member) * owned
    label_ids = first_label + jnp.arange(owned, dtype=jnp.int32)
    balance = balances(label_counts)
    replaced = jnp.any(
        refresh_rows[:, None] == jnp.arange(owned, dtype=jnp.int32)[None, :], axis=0
    )
    kept = jnp.where(replaced, 0.0, balance)
    early_slopes, early_loss = focal(queries, label_table, positives, label_ids, kept, root)
    query_part = jnp.dot(early_slopes, label_table, preferred_element_type=jnp.float32) / root
    query_sum, loss_sum, summed_weight = lax.psum(
        (query_part, early_loss, jnp.sum(balance)), ("dp", "mp")
    )
    new_ids = lax.all_gather(first_label + refresh_rows, ("dp", "mp"), axis=0, tiled=True)
    new_balance = lax.all_gather(balance[refresh_rows], ("dp", "mp"), axis=0, tiled=True)
    refreshed_all = lax.all_gather(refreshed, ("dp", "mp"), axis=0, tiled=True)
    late_slopes, late_loss = focal(queries, refreshed_all, positives, new_ids, new_balance, root)
    query_late = jnp.dot(late_slopes, refreshed_all, preferred_element_type=jnp.float32) / root
    own_late = lax.dynamic_slice_in_dim(
        late_slopes, (lax.axis_index("dp") * members + member) * share, share, 1
    )
    slopes = early_slopes.at[:, refresh_rows].set(own_late)
    label_part = (
        lax.dot_general(
            slopes, queries, (((0,), (0,)), ((), ())), preferred_element_type=jnp.float32
        )
        / root
    )
    total_labels = owned * groups * members
    factor = total_labels / summed_weight
    loss = factor * (loss_sum + late_loss) / (queries.shape[0] * total_labels)
    return (factor * label_part, factor * (query_sum + query_late), loss)


def balances(label_counts):
    return (1.0 - focal_beta) / -jnp.expm1(
        label_counts.astype(jnp.float32) * math.log(focal_beta)
    )


def focal(queries, table, positives, label_ids, balance, root):
    logits = (
        lax.dot_general(
            queries, table, (((1,), (1,)), ((), ())), preferred_element_type=jnp.float32
        )
        / root
    )
    matched = jnp.any(positives[:, :, None] == label_ids[None, None, :], axis=1)
    signs = jnp.where(matched, 1.0, -1.0)
    margin = signs * logits
    missed = jax.nn.sigmoid(-margin)
    softened = jax.nn.softplus(-margin)
    loss = jnp.sum(balance[None, :] * missed * missed * softened)
    slopes = (
        balance[None, :]
        * signs
        * (-(missed * missed) * (2.0 * jax.nn.sigmoid(margin) * softened + missed))
    ).astype(jnp.bfloat16)
    return slopes, loss


def solution(mesh):
    in_specs = (
        P("dp", None),
        P("dp", None),
        P(),
        P("dp", "mp"),
        P("dp", "mp"),
        P("dp", "mp"),
        P("dp", "mp"),
        P(("dp", "mp"), None),
        P(("dp", "mp")),
        P(("dp", "mp")),
        P(),
        P(),
    )
    out_specs = (P(("dp", "mp"), None), P(), P())
    return jax.shard_map(shards, mesh=mesh, in_specs=in_specs, out_specs=out_specs, check_vma=False)
```

```python
import functools
import math

import jax
import jax.numpy as jnp
from jax import lax
from jax.experimental import pallas as pl
from jax.experimental.pallas import tpu as pltpu
from jax.sharding import PartitionSpec as P

MESH = pl.DeviceIdType.MESH
SIDES = 2

HEAD_WIDTH = 128


rope_theta = 1000000.0
norm_eps = 1e-06
focal_beta = 0.9999


def rotary(values, head_size):
    length = values.shape[1]
    half = head_size // 2
    frequency = rope_theta ** (-2.0 * jnp.arange(half, dtype=jnp.float32) / head_size)
    angles = jnp.arange(length, dtype=jnp.float32)[:, None] * frequency[None, :]
    cosine = jnp.concatenate([jnp.cos(angles), jnp.cos(angles)], axis=1)[None, :, None, :]
    sine = jnp.concatenate([jnp.sin(angles), jnp.sin(angles)], axis=1)[None, :, None, :]
    turned = jnp.concatenate([-values[..., half:], values[..., :half]], axis=-1)
    return values * cosine + turned * sine


def attend(query_rows, key_rows, value_rows, text_ids, head_size):
    texts, length = text_ids.shape
    kv_heads = key_rows.shape[1] // head_size
    repeat = query_rows.shape[1] // head_size // kv_heads
    query_r = query_rows.reshape(texts, length, kv_heads, repeat, head_size)
    key_r = key_rows.reshape(texts, length, kv_heads, head_size)
    value_r = value_rows.reshape(texts, length, kv_heads, head_size)
    scores = jnp.einsum(
        "ntgrd,nsgd->ngrts", query_r, key_r, preferred_element_type=jnp.float32
    ) / math.sqrt(head_size)
    causal = jnp.arange(length)[:, None] >= jnp.arange(length)[None, :]
    allowed = causal[None, None, None, :, :] & (text_ids != 0)[:, None, None, None, :]
    weights = jnp.where(allowed, jnp.exp(scores), 0.0)
    probs = (weights / jnp.sum(weights, axis=-1, keepdims=True)).astype(jnp.bfloat16)
    mixed = jnp.einsum("ngrts,nsgd->ntgrd", probs, value_r, preferred_element_type=jnp.float32)
    return mixed.reshape(texts * length, -1).astype(jnp.bfloat16)


def remote(source, target, send, receive, device):
    return pltpu.make_async_remote_copy(
        src_ref=source,
        dst_ref=target,
        send_sem=send,
        recv_sem=receive,
        device_id=device,
        device_id_type=MESH,
    )


def each(low, high, body):
    def run(index, carry):
        body(index)
        return carry

    lax.fori_loop(low, high, run, 0)


def slopes_of(logits, positives, label_ids, balance):
    matched = positives[:, 0:1] == label_ids
    for index in range(1, positives.shape[1]):
        matched = matched | (positives[:, index : index + 1] == label_ids)
    signs = jnp.where(matched, 1.0, -1.0)
    margin = signs * logits
    small = jnp.exp(-jnp.abs(margin))
    larger, smaller = 1.0 / (1.0 + small), small / (1.0 + small)
    missed = jnp.where(margin >= 0.0, smaller, larger)
    hit = jnp.where(margin >= 0.0, larger, smaller)
    softened = jnp.maximum(-margin, 0.0) + jnp.log1p(small)
    loss = jnp.sum(balance * missed * missed * softened)
    made = balance * signs * (-(missed * missed) * (2.0 * hit * softened + missed))
    return made.astype(jnp.bfloat16), loss


def spread(groups, members, blocks, group_sem, far_sem, core_sem, relay_sem, arrived):
    group, member = lax.axis_index("dp"), lax.axis_index("mp")
    far = lax.rem(member + 2, members)
    core = member + 1 - 2 * lax.rem(member, 2)
    far_core = lax.rem(core + 2, members)

    def copy(at, slot, sems, index, device):
        return remote(blocks.at[slot], blocks.at[slot], sems.at[index], arrived.at[slot], device)

    def forward(at):
        slot = at * members + member
        copy(at, slot, far_sem, at, (group, far)).start()
        copy(at, slot, core_sem, at, (group, core)).start()

    def send(step):
        slot = group * members + member
        copy(group, slot, group_sem, step, (lax.rem(group + step, groups), member)).start()

    def pass_on(step):
        at = lax.rem(group + groups - step, groups)
        slot = at * members + member
        copy(at, slot, group_sem, step, (at, member)).wait_recv()
        forward(at)

    def relay(step):
        at = lax.rem(group + groups - step, groups)
        slot = at * members + far
        copy(at, slot, far_sem, at, (group, far)).wait_recv()
        copy(at, slot, relay_sem, at, (group, core)).start()

    def finish(at):
        copy(at, at * members + core, core_sem, at, (group, core)).wait_recv()
        copy(at, at * members + far_core, relay_sem, at, (group, core)).wait_recv()
        copy(at, at * members + member, far_sem, at, (group, far)).wait_send()
        copy(at, at * members + member, core_sem, at, (group, core)).wait_send()
        copy(at, at * members + far, relay_sem, at, (group, core)).wait_send()

    def sent(step):
        slot = group * members + member
        copy(group, slot, group_sem, step, (lax.rem(group + step, groups), member)).wait_send()

    def start():
        each(1, groups, send)
        forward(group)

    def end():
        each(1, groups, pass_on)
        each(0, groups, relay)
        each(0, groups, finish)
        each(1, groups, sent)

    return start, end


def spread_sems(groups, members):
    return [
        pltpu.SemaphoreType.DMA((groups,)),
        pltpu.SemaphoreType.DMA((groups,)),
        pltpu.SemaphoreType.DMA((groups,)),
        pltpu.SemaphoreType.DMA((groups,)),
        pltpu.SemaphoreType.DMA((groups * members,)),
    ]


def project_kernel(
    groups,
    members,
    states_far,
    q_weight,
    key_matrix,
    value_matrix,
    queries_far,
    table_far,
    gain,
    positives,
    label_ids,
    kept,
    meta,
    ids,
    turns,
    pooled,
    base,
    slopes,
    blocks,
    states,
    queries,
    table,
    raw,
    pools,
    weights,
    normed,
    part,
    got,
    sums,
    terms,
    local_sem,
    short_sem,
    up_sem,
    down_sem,
    side_sem,
    landed,
    s1,
    r1,
    s2,
    r2,
    *sems,
):
    group, member = lax.axis_index("dp"), lax.axis_index("mp")
    own = group * members + member
    depth = groups // SIDES
    level, side = group // SIDES, lax.rem(group, SIDES)
    block = table.shape[1] // groups
    rows = queries.shape[0] // members
    heads, kv = q_weight.shape[1], key_matrix.shape[1]
    barrier = pltpu.get_barrier_semaphore()

    def greet_member(step):
        peer = lax.rem(member + step, members)
        pl.semaphore_signal(barrier, inc=1, device_id=(group, peer), device_id_type=MESH)

    def greet_group(step):
        peer = lax.rem(group + step, groups)
        pl.semaphore_signal(barrier, inc=1, device_id=(peer, member), device_id_type=MESH)

    held = weights.at[group]
    fetches = [
        pltpu.make_async_copy(source, target, local_sem.at[index])
        for index, (source, target) in enumerate(
            (
                (q_weight, held.at[:, pl.ds(0, heads)]),
                (key_matrix, held.at[:, pl.ds(heads, kv)]),
                (value_matrix, held.at[:, pl.ds(heads + kv, kv)]),
                (queries_far, queries),
                (table_far, table),
                (states_far, states),
            )
        )
    ]
    for fetch in fetches:
        fetch.start()
    each(1, members, greet_member)
    each(1, groups, greet_group)
    for fetch in fetches[:3]:
        fetch.wait()
    pl.semaphore_wait(barrier, groups + members - 2)

    def weight_copy(slot, sem, peer):
        return remote(
            weights.at[slot], weights.at[slot], sem.at[slot], landed.at[slot], (peer, member)
        )

    def up(slot):
        return weight_copy(slot, up_sem, group + SIDES)

    def down(slot):
        return weight_copy(slot, down_sem, group - SIDES)

    partner = level + 1 - 2 * lax.rem(level, 2)
    middle = block // 32 * 16

    def across(at, from_side, act):
        slot = at * SIDES + from_side
        peer = level * SIDES + 1 - side

        @pl.when(at != partner)
        def _():
            act(weight_copy(slot, side_sem, peer))

        @pl.when(at == partner)
        def _():
            rest = weights.at[slot, pl.ds(middle, block - middle), :]
            act(remote(rest, rest, side_sem.at[slot], landed.at[slot], (peer, member)))

    def shortcut(at):
        first = weights.at[at * SIDES + 1 - side, pl.ds(0, middle), :]
        peer = partner * SIDES + side
        return remote(first, first, short_sem.at[0], short_sem.at[1], (peer, member))

    def begin(copy):
        copy.start()

    def arrive(copy):
        copy.wait_recv()

    def leave(copy):
        copy.wait_send()

    def travel(step):
        @pl.when(level >= step)
        def _():
            slot = group - step * SIDES
            if step > 0:
                weight_copy(slot, down_sem, group - SIDES).wait_recv()

            @pl.when(level < depth - 1)
            def _():
                up(slot).start()

            across(level - step, side, begin)

        if step == 0:

            @pl.when(level > 0)
            def _():
                down(group).start()

        else:

            @pl.when(level + step < depth)
            def _():
                slot = group + step * SIDES
                weight_copy(slot, up_sem, group + SIDES).wait_recv()

                @pl.when(level > 0)
                def _():
                    down(slot).start()

                across(level + step, side, begin)

    tokens = states.shape[0]
    tile = 128 if tokens % 128 == 0 else tokens

    def multiply(slot):
        def some(index):
            at = pl.ds(pl.multiple_of(index * tile, tile), tile)
            raw[at, :] += jnp.dot(
                normed[slot, at, :], weights[slot], preferred_element_type=jnp.float32
            )

        each(0, tokens // tile, some)

    def multiply_step(step):
        @pl.when(level >= step)
        def _():
            multiply(group - step * SIDES)

        if step > 0:

            @pl.when(level + step < depth)
            def _():
                multiply(group + step * SIDES)

    def multiply_across(step):
        def one(at):
            if step > 0:
                across(at, 1 - side, arrive)
            if step == 1:

                @pl.when(at == partner)
                def _():
                    shortcut(at).wait_recv()

            multiply(at * SIDES + 1 - side)

        @pl.when(level >= step)
        def _():
            one(level - step)

        if step > 0:

            @pl.when(level + step < depth)
            def _():
                one(level + step)

    travel(0)
    for fetch in fetches[3:]:
        fetch.wait()

    root = math.sqrt(table.shape[1])
    logits = (
        lax.dot_general(
            queries[...],
            table[...],
            (((1,), (1,)), ((), ())),
            preferred_element_type=jnp.float32,
        )
        / root
    )
    early, loss = slopes_of(logits, positives[...], label_ids[...], kept[...])
    slopes[...] = early
    for at in range(groups):
        part[at] = (
            jnp.dot(
                early,
                table[:, at * block : (at + 1) * block],
                preferred_element_type=jnp.float32,
            )
            / root
        )

    def member_copy(step):
        peer = lax.rem(member + step, members)
        start = pl.multiple_of(peer * rows, rows)
        return remote(
            part.at[:, pl.ds(start, rows), :],
            got.at[member],
            s1.at[step],
            r1.at[member],
            (group, peer),
        )

    def member_wait(step):
        source = lax.rem(member + members - step, members)
        remote(
            got.at[source], got.at[source], s1.at[step], r1.at[source], (group, source)
        ).wait_recv()

    each(1, members, lambda step: member_copy(step).start())

    def normalize(index):
        at = pl.ds(pl.multiple_of(index * 64, 64), 64)
        wide = states[at, :].astype(jnp.float32)
        scaled = lax.rsqrt(jnp.mean(wide * wide, axis=1, keepdims=True) + norm_eps)
        ready = (wide * scaled * gain[...]).astype(jnp.bfloat16)
        for piece in range(groups):
            normed[piece, at, :] = ready[:, piece * block : (piece + 1) * block]

    each(0, tokens // 64, normalize)
    texts, length = pooled.shape[0], tokens // pooled.shape[0]
    chunk, share = tokens // members, texts // members

    def living(index):
        live = ids[index] != 0
        row = lax.broadcasted_iota(jnp.int32, (share, chunk), 0)
        column = lax.broadcasted_iota(jnp.int32, (share, chunk), 1)
        chosen = jnp.where((lax.div(column, length) == row) & live, 1.0, 0.0)
        return chosen.astype(jnp.bfloat16), jnp.sum(chosen, axis=1, keepdims=True)

    chosen, counted = living(member)
    mine = pl.ds(pl.multiple_of(member * chunk, chunk), chunk)
    for at in range(groups):
        base[at] = (
            jnp.dot(
                chosen,
                states[mine, at * block : (at + 1) * block],
                preferred_element_type=jnp.float32,
            )
            / counted
        )
    raw[...] = jnp.zeros_like(raw)
    multiply_step(0)
    travel(1)
    across(level, 1 - side, arrive)
    shortcut(level).start()
    each(1, members, member_wait)
    first = pl.multiple_of(member * rows, rows)

    def add_members(at):
        total = part[at, pl.ds(first, rows), :]
        for step in range(1, members):
            total = total + got[lax.rem(member + step, members), at]
        sums[at] = total

    each(0, groups, add_members)

    def group_copy(step):
        peer = lax.rem(group + step, groups)
        return remote(sums.at[peer], terms.at[group], s2.at[step], r2.at[group], (peer, member))

    def group_wait(step):
        source = lax.rem(group + groups - step, groups)
        remote(
            terms.at[source], terms.at[source], s2.at[step], r2.at[source], (source, member)
        ).wait_recv()

    each(1, groups, lambda step: group_copy(step).start())
    multiply_step(1)
    multiply_across(0)
    travel(2)
    each(1, groups, group_wait)
    total = sums[group]
    for step in range(1, groups):
        total = total + terms[lax.rem(group + step, groups)]
    blocks[own, :rows] = total
    line = lax.broadcasted_iota(jnp.int32, meta.shape, 0)
    blocks[own, rows:] = jnp.where(line == 3, loss, meta[...])
    start, end = spread(groups, members, blocks, *sems)
    start()
    multiply_step(2)
    multiply_across(1)
    for step in range(3, depth):
        travel(step)
        multiply_step(step)
    end()
    for step in range(2, depth):
        multiply_across(step)

    def attend_some(index):
        at = pl.ds(pl.multiple_of(index * chunk, chunk), chunk)

        def rotate(values):
            turned = pltpu.roll(values, HEAD_WIDTH // 2, 1)
            return (values * turns[0] + turned * turns[1]).astype(jnp.bfloat16)

        row = lax.broadcasted_iota(jnp.int32, (chunk, chunk), 0)
        column = lax.broadcasted_iota(jnp.int32, (chunk, chunk), 1)
        allowed = (lax.div(row, length) == lax.div(column, length)) & (column <= row)
        allowed = allowed & (ids[index] != 0)
        chosen, counted = living(index)
        repeat = heads // kv
        out = pl.ds(pl.multiple_of(index * share, share), share)
        for head in range(heads // HEAD_WIDTH):
            if head % repeat == 0:
                start = heads + head // repeat * HEAD_WIDTH
                keys = rotate(raw[at, start : start + HEAD_WIDTH])
                values = raw[at, start + kv : start + kv + HEAD_WIDTH].astype(jnp.bfloat16)
            columns = slice(head * HEAD_WIDTH, (head + 1) * HEAD_WIDTH)
            scores = lax.dot_general(
                rotate(raw[at, columns]),
                keys,
                (((1,), (1,)), ((), ())),
                preferred_element_type=jnp.float32,
            ) / math.sqrt(HEAD_WIDTH)
            made = jnp.where(allowed, jnp.exp(scores), 0.0)
            probs = (made / jnp.sum(made, axis=1, keepdims=True)).astype(jnp.bfloat16)
            mixed = jnp.dot(probs, values, preferred_element_type=jnp.float32)
            pools[out, columns] = (
                jnp.dot(chosen, mixed.astype(jnp.bfloat16), preferred_element_type=jnp.float32)
                / counted
            )

    each(0, members, attend_some)
    pooled[...] = pools[...].astype(jnp.bfloat16)

    each(1, members, lambda step: member_copy(step).wait_send())
    each(1, groups, lambda step: group_copy(step).wait_send())

    def weights_sent(at):
        slot = at * SIDES + side
        across(at, side, leave)

        @pl.when((at <= level) & (level < depth - 1))
        def _():
            up(slot).wait_send()

        @pl.when((at >= level) & (level > 0))
        def _():
            down(slot).wait_send()

    each(0, depth, weights_sent)
    shortcut(level).wait_send()


def project(
    states,
    q_weight,
    key_matrix,
    value_matrix,
    queries,
    table,
    gain,
    positives,
    label_ids,
    kept,
    meta,
    ids,
    turns,
    groups,
    members,
):
    tokens, width = states.shape
    batch = queries.shape[0]
    heads = q_weight.shape[1]
    texts = members * (meta.shape[0])
    rows, block = batch // members, width // groups
    columns = heads + key_matrix.shape[1] + value_matrix.shape[1]
    group_sems = [pltpu.SemaphoreType.DMA((groups,))]
    return pl.pallas_call(
        functools.partial(project_kernel, groups, members),
        out_shape=(
            jax.ShapeDtypeStruct((texts, heads), jnp.bfloat16),
            jax.ShapeDtypeStruct((groups, texts // members, block), jnp.float32),
            jax.ShapeDtypeStruct((batch, table.shape[0]), jnp.bfloat16),
            jax.ShapeDtypeStruct(
                (groups * members, rows + meta.shape[0], block), jnp.float32
            ),
        ),
        in_specs=[pl.BlockSpec(memory_space=pl.ANY)] * 6
        + [pl.BlockSpec(memory_space=pltpu.VMEM)] * 7,
        out_specs=tuple([pl.BlockSpec(memory_space=pltpu.VMEM)] * 4),
        scratch_shapes=[
            pltpu.VMEM(states.shape, jnp.bfloat16),
            pltpu.VMEM(queries.shape, jnp.bfloat16),
            pltpu.VMEM(table.shape, jnp.bfloat16),
            pltpu.VMEM((tokens, columns), jnp.float32),
            pltpu.VMEM((texts, heads), jnp.float32),
            pltpu.VMEM((groups, block, columns), jnp.bfloat16),
            pltpu.VMEM((groups, tokens, block), jnp.bfloat16),
            pltpu.VMEM((groups, batch, block), jnp.float32),
            pltpu.VMEM((members, groups, rows, block), jnp.float32),
            pltpu.VMEM((groups, rows, block), jnp.float32),
            pltpu.VMEM((groups, rows, block), jnp.float32),
            pltpu.SemaphoreType.DMA((6,)),
            pltpu.SemaphoreType.DMA((2,)),
            *(group_sems * 4),
            pltpu.SemaphoreType.DMA((members,)),
            pltpu.SemaphoreType.DMA((members,)),
            *(group_sems * 2),
            *spread_sems(groups, members),
        ],
        compiler_params=pltpu.CompilerParams(
            collective_id=0, has_side_effects=True, vmem_limit_bytes=48 << 20
        ),
        name="project",
    )(
        states,
        q_weight,
        key_matrix,
        value_matrix,
        queries,
        table,
        gain,
        positives,
        label_ids,
        kept,
        meta,
        ids,
        turns,
    )


def tail_kernel(
    groups,
    members,
    owned,
    pooled,
    weight,
    base,
    queries,
    positives,
    early,
    reduced,
    query_out,
    slopes,
    scalars,
    blocks,
    pool,
    terms,
    parts,
    rows_wide,
    s1,
    r1,
    s2,
    r2,
    *sems,
):
    group, member = lax.axis_index("dp"), lax.axis_index("mp")
    own = group * members + member
    devices = groups * members
    share = terms.shape[1]
    barrier = pltpu.get_barrier_semaphore()

    def greet(step):
        peer = lax.rem(own + step, devices)
        pl.semaphore_signal(
            barrier,
            inc=1,
            device_id=(peer // members, lax.rem(peer, members)),
            device_id_type=MESH,
        )

    each(1, devices, greet)
    pl.semaphore_wait(barrier, devices - 1)

    def pool_copy(step):
        peer = lax.rem(group + step, groups)
        return remote(pooled, pool.at[group], s1.at[step], r1.at[group], (peer, member))

    def part_copy(owner_group, owner_member):
        slot = owner_group * members + owner_member
        return remote(
            terms.at[slot], parts.at[own], s2.at[slot], r2.at[own], (owner_group, owner_member)
        )

    def product(at, rows):
        made = jnp.dot(rows, weight[...], preferred_element_type=jnp.float32)
        for index in range(members):
            terms[at * members + index] = made[index * share : (index + 1) * share]

    def project(step):
        at = lax.rem(group + groups - step, groups)
        remote(pooled, pool.at[at], s1.at[step], r1.at[at], (at, member)).wait_recv()
        product(at, pool[at])
        each(0, members, lambda index: part_copy(at, index).start())

    each(1, groups, lambda step: pool_copy(step).start())
    product(group, pooled[...])
    each(1, members, lambda step: part_copy(group, lax.rem(member + step, members)).start())
    parts[own] = terms[own]
    each(1, groups, project)

    def part_wait(step):
        source = lax.rem(own + devices - step, devices)
        remote(
            terms.at[source],
            parts.at[source],
            s2.at[source],
            r2.at[source],
            (source // members, lax.rem(source, members)),
        ).wait_recv()

    each(1, devices, part_wait)
    rows = []
    for at in range(groups):
        total = base[at]
        for index in range(members):
            total = total + parts[at * members + index]
        rows.append(total)
    blocks[own] = jnp.concatenate(rows, axis=0).astype(jnp.bfloat16)
    start, end = spread(groups, members, blocks, *sems)
    start()
    texts = devices * share
    block = base.shape[2]
    batch = queries.shape[0]
    height = batch // members
    notes = reduced[0, height:, :]
    for at in range(1, devices):
        notes = notes + reduced[at, height:, :]
    new_ids = notes[0:1, :texts].astype(jnp.int32)
    scalars[...] = notes[:, :128]
    end()

    def widen(at):
        wide = blocks[at].astype(jnp.float32)
        for piece in range(groups):
            rows_wide[piece, pl.ds(pl.multiple_of(at * share, share), share), :] = wide[
                piece * share : (piece + 1) * share
            ]

    each(0, devices, widen)
    root = math.sqrt(groups * block)
    logits = jnp.zeros((batch, texts), jnp.float32)
    for piece in range(groups):
        logits = logits + lax.dot_general(
            queries[:, piece * block : (piece + 1) * block],
            rows_wide[piece].astype(jnp.bfloat16),
            (((1,), (1,)), ((), ())),
            preferred_element_type=jnp.float32,
        )
    late, loss = slopes_of(logits / root, positives[...], new_ids, notes[1:2, :texts])
    line = lax.broadcasted_iota(jnp.int32, scalars.shape, 0)
    scalars[...] = scalars[...] + jnp.where(line == 3, loss, 0.0)
    for piece in range(groups):
        made = (
            jnp.dot(
                late, rows_wide[piece].astype(jnp.bfloat16), preferred_element_type=jnp.float32
            )
            / root
        )
        for index in range(members):
            query_out[
                index * height : (index + 1) * height, piece * block : (piece + 1) * block
            ] = (
                made[index * height : (index + 1) * height]
                + reduced[piece * members + index, :height, :]
            )
    labels = own * owned + lax.broadcasted_iota(jnp.int32, (owned, texts), 0)
    place = jnp.where(labels == new_ids, 1.0, 0.0).astype(jnp.bfloat16)
    moved = lax.dot_general(
        late, place, (((1,), (1,)), ((), ())), preferred_element_type=jnp.float32
    )
    slopes[...] = (early[...].astype(jnp.float32) + moved).astype(jnp.bfloat16)
    each(1, groups, lambda step: pool_copy(step).wait_send())

    def part_sent(step):
        slot = lax.rem(own + step, devices)
        part_copy(slot // members, lax.rem(slot, members)).wait_send()

    each(1, devices, part_sent)


def tail(pooled, weight, base, queries, positives, early, reduced, groups, members):
    texts, heads = pooled.shape
    block = weight.shape[1]
    share = texts // members
    devices = groups * members
    return pl.pallas_call(
        functools.partial(tail_kernel, groups, members, early.shape[1]),
        out_shape=(
            jax.ShapeDtypeStruct(queries.shape, jnp.float32),
            jax.ShapeDtypeStruct(early.shape, jnp.bfloat16),
            jax.ShapeDtypeStruct((8, 128), jnp.float32),
        ),
        in_specs=[pl.BlockSpec(memory_space=pltpu.VMEM)] * 7,
        out_specs=tuple([pl.BlockSpec(memory_space=pltpu.VMEM)] * 3),
        scratch_shapes=[
            pltpu.VMEM((devices, groups * share, block), jnp.bfloat16),
            pltpu.VMEM((groups, texts, heads), jnp.bfloat16),
            pltpu.VMEM((devices, share, block), jnp.float32),
            pltpu.VMEM((devices, share, block), jnp.float32),
            pltpu.VMEM((groups, devices * share, block), jnp.float32),
            pltpu.SemaphoreType.DMA((groups,)),
            pltpu.SemaphoreType.DMA((groups,)),
            pltpu.SemaphoreType.DMA((devices,)),
            pltpu.SemaphoreType.DMA((devices,)),
            *spread_sems(groups, members),
        ],
        compiler_params=pltpu.CompilerParams(
            collective_id=1, has_side_effects=True, vmem_limit_bytes=40 << 20
        ),
        name="tail",
    )(pooled, weight, base, queries, positives, early, reduced)


def kernels_fit(groups, members, width, share):
    lanes = -(-(width // groups) // 128) * 128
    return (
        members == 4
        and share == 8
        and groups % (2 * SIDES) == 0
        and groups * members * share <= width // groups
        and groups * members * groups * share * lanes * 2 < 8 << 20
    )


def shards(
    hidden_states,
    token_ids,
    norm_gain,
    q_weight,
    key_matrix,
    value_matrix,
    out_weight,
    label_table,
    refresh_rows,
    label_counts,
    queries,
    positives,
):
    width = hidden_states.shape[1]
    texts, length = token_ids.shape
    groups = lax.axis_size("dp")
    members = lax.axis_size("mp")
    share = texts // members
    if not kernels_fit(groups, members, width, share):
        return plain_shards(
            hidden_states,
            token_ids,
            norm_gain,
            q_weight,
            key_matrix,
            value_matrix,
            out_weight,
            label_table,
            refresh_rows,
            label_counts,
            queries,
            positives,
        )
    block = width // groups
    root = math.sqrt(width)
    owned = label_table.shape[0]
    own = lax.axis_index("dp") * members + lax.axis_index("mp")
    first_label = own * owned
    label_ids = first_label + jnp.arange(owned, dtype=jnp.int32)
    balance = balances(label_counts)
    replaced = refresh_rows[:, None] == jnp.arange(owned, dtype=jnp.int32)[None, :]
    kept = jnp.where(jnp.any(replaced, axis=0), 0.0, balance)
    lanes = jnp.arange(block, dtype=jnp.int32)
    here = (lanes // share) == own
    spot = lanes % share
    picked = (spot[None, :] == jnp.arange(share, dtype=jnp.int32)[:, None]) & here[None, :]
    new_balance = jnp.sum(jnp.where(replaced, balance[None, :], 0.0), axis=1)
    new_ids = (first_label + refresh_rows).astype(jnp.float32)
    meta = jnp.concatenate(
        [
            jnp.sum(jnp.where(picked, new_ids[:, None], 0.0), axis=0, keepdims=True),
            jnp.sum(jnp.where(picked, new_balance[:, None], 0.0), axis=0, keepdims=True),
            jnp.broadcast_to(jnp.sum(balance), (1, block)),
            jnp.zeros((5, block), jnp.float32),
        ],
        axis=0,
    )
    half = HEAD_WIDTH // 2
    frequency = rope_theta ** (-2.0 * jnp.arange(half, dtype=jnp.float32) / HEAD_WIDTH)
    places = jnp.arange(share * length, dtype=jnp.int32) % length
    angles = places.astype(jnp.float32)[:, None] * frequency[None, :]
    cosine, sine = jnp.cos(angles), jnp.sin(angles)
    turns = jnp.stack(
        [
            jnp.concatenate([cosine, cosine], axis=1),
            jnp.concatenate([-sine, sine], axis=1),
        ]
    )
    pooled, base, early, reduced = project(
        hidden_states,
        q_weight,
        key_matrix,
        value_matrix,
        queries,
        label_table,
        norm_gain[None, :],
        positives,
        label_ids[None, :],
        kept[None, :],
        meta,
        token_ids.reshape(members, 1, share * length),
        turns,
        groups,
        members,
    )
    query_sum, slopes, scalars = tail(
        pooled, out_weight.T, base, queries, positives, early, reduced, groups, members
    )
    total_labels = owned * groups * members
    factor = total_labels / scalars[2, 0]
    loss = factor * scalars[3, 0] / (queries.shape[0] * total_labels)
    label_part = (
        lax.dot_general(
            slopes, queries, (((0,), (0,)), ((), ())), preferred_element_type=jnp.float32
        )
        / root
    )
    return (factor * label_part, factor * query_sum, loss)


def plain_shards(
    hidden_states,
    token_ids,
    norm_gain,
    q_weight,
    key_matrix,
    value_matrix,
    out_weight,
    label_table,
    refresh_rows,
    label_counts,
    queries,
    positives,
):
    width = hidden_states.shape[1]
    group_tokens = hidden_states.shape[0]
    texts, length = token_ids.shape
    states = hidden_states.astype(jnp.float32)
    scaled = lax.rsqrt(jnp.mean(states * states, axis=1, keepdims=True) + norm_eps)
    normed = (states * scaled * norm_gain).astype(jnp.bfloat16)
    heads = q_weight.shape[1]
    kv = key_matrix.shape[1]
    weights = lax.all_gather(
        jnp.concatenate([q_weight, key_matrix, value_matrix], axis=1), "dp", axis=0, tiled=True
    )
    raw = jnp.dot(normed, weights, preferred_element_type=jnp.float32)
    query_raw = raw[:, :heads]
    key_raw = raw[:, heads : heads + kv]
    value_raw = raw[:, heads + kv :]
    queries_rot = (
        rotary(query_raw.reshape(texts, length, -1, HEAD_WIDTH), HEAD_WIDTH)
        .reshape(group_tokens, -1)
        .astype(jnp.bfloat16)
    )
    rotary_keys = (
        rotary(key_raw.reshape(texts, length, -1, HEAD_WIDTH), HEAD_WIDTH)
        .reshape(group_tokens, -1)
        .astype(jnp.bfloat16)
    )
    values_rot = value_raw.astype(jnp.bfloat16)
    attended = attend(queries_rot, rotary_keys, values_rot, token_ids, HEAD_WIDTH)
    live = (token_ids != 0).astype(jnp.float32)
    counted = jnp.sum(live, axis=1, keepdims=True)
    pooled = (
        jnp.sum(attended.astype(jnp.float32).reshape(texts, length, -1) * live[:, :, None], axis=1)
        / counted
    ).astype(jnp.bfloat16)
    groups = lax.axis_size("dp")
    members = lax.axis_size("mp")
    share = texts // members
    member = lax.axis_index("mp")
    live_own = lax.dynamic_slice_in_dim(live, member * share, share, 0)
    states_own = lax.dynamic_slice_in_dim(
        hidden_states, member * share * length, share * length, 0
    ).reshape(share, length, width)
    counted_own = jnp.sum(live_own, axis=1, keepdims=True)
    base_own = (
        jnp.sum(states_own.astype(jnp.float32) * live_own[:, :, None], axis=1) / counted_own
    )
    pooled_all = lax.all_gather(pooled, "dp", axis=0, tiled=True)
    terms = lax.dot_general(
        pooled_all, out_weight, (((1,), (1,)), ((), ())), preferred_element_type=jnp.float32
    ).reshape(groups, members, share, -1)
    mine = lax.psum_scatter(terms, "mp", scatter_dimension=1, tiled=True)
    mine = mine.reshape(groups, share, -1)
    swapped = lax.all_to_all(mine, "dp", 0, 0, tiled=True)
    projected = jnp.swapaxes(swapped, 0, 1).reshape(share, width)
    refreshed = (base_own + projected).astype(jnp.bfloat16)

    root = math.sqrt(width)
    owned = label_table.shape[0]
    first_label = (lax.axis_index("dp") * members + member) * owned
    label_ids = first_label + jnp.arange(owned, dtype=jnp.int32)
    balance = balances(label_counts)
    replaced = jnp.any(
        refresh_rows[:, None] == jnp.arange(owned, dtype=jnp.int32)[None, :], axis=0
    )
    kept = jnp.where(replaced, 0.0, balance)
    early_slopes, early_loss = focal(queries, label_table, positives, label_ids, kept, root)
    query_part = jnp.dot(early_slopes, label_table, preferred_element_type=jnp.float32) / root
    query_sum, loss_sum, summed_weight = lax.psum(
        (query_part, early_loss, jnp.sum(balance)), ("dp", "mp")
    )
    new_ids = lax.all_gather(first_label + refresh_rows, ("dp", "mp"), axis=0, tiled=True)
    new_balance = lax.all_gather(balance[refresh_rows], ("dp", "mp"), axis=0, tiled=True)
    refreshed_all = lax.all_gather(refreshed, ("dp", "mp"), axis=0, tiled=True)
    late_slopes, late_loss = focal(queries, refreshed_all, positives, new_ids, new_balance, root)
    query_late = jnp.dot(late_slopes, refreshed_all, preferred_element_type=jnp.float32) / root
    own_late = lax.dynamic_slice_in_dim(
        late_slopes, (lax.axis_index("dp") * members + member) * share, share, 1
    )
    slopes = early_slopes.at[:, refresh_rows].set(own_late)
    label_part = (
        lax.dot_general(
            slopes, queries, (((0,), (0,)), ((), ())), preferred_element_type=jnp.float32
        )
        / root
    )
    total_labels = owned * groups * members
    factor = total_labels / summed_weight
    loss = factor * (loss_sum + late_loss) / (queries.shape[0] * total_labels)
    return (factor * label_part, factor * (query_sum + query_late), loss)


def balances(label_counts):
    return (1.0 - focal_beta) / -jnp.expm1(
        label_counts.astype(jnp.float32) * math.log(focal_beta)
    )


def focal(queries, table, positives, label_ids, balance, root):
    logits = (
        lax.dot_general(
            queries, table, (((1,), (1,)), ((), ())), preferred_element_type=jnp.float32
        )
        / root
    )
    matched = jnp.any(positives[:, :, None] == label_ids[None, None, :], axis=1)
    signs = jnp.where(matched, 1.0, -1.0)
    margin = signs * logits
    missed = jax.nn.sigmoid(-margin)
    softened = jax.nn.softplus(-margin)
    loss = jnp.sum(balance[None, :] * missed * missed * softened)
    slopes = (
        balance[None, :]
        * signs
        * (-(missed * missed) * (2.0 * jax.nn.sigmoid(margin) * softened + missed))
    ).astype(jnp.bfloat16)
    return slopes, loss


def solution(mesh):
    in_specs = (
        P("dp", None),
        P("dp", None),
        P(),
        P("dp", "mp"),
        P("dp", "mp"),
        P("dp", "mp"),
        P("dp", "mp"),
        P(("dp", "mp"), None),
        P(("dp", "mp")),
        P(("dp", "mp")),
        P(),
        P(),
    )
    out_specs = (P(("dp", "mp"), None), P(), P())
    return jax.shard_map(shards, mesh=mesh, in_specs=in_specs, out_specs=out_specs, check_vma=False)
```
